32 devices in a mesh: wide: 8 (over z, x), narrow: 4 (over y, core).
Axes of the slice: x: 2, y: 2, z: 4, core: 2. Of those that a mesh axis runs over, the one named last changes fastest.
Arguments:
- state: float32 [4, 512, 512], P('narrow'), may hold values from -1.5 to 1.5
- left_env: float32 [32, 4, 512, 512], P('wide', 'narrow')
- right_env: float32 [32, 4, 512, 512], P('wide', 'narrow')
- left_sizes: int32 [4], replicated, may hold values from 1 to 512, 1536 in all
- right_sizes: int32 [4], replicated, may hold values from 1 to 512, 1536 in all
- channel_charge: int32 [32], P('wide'), may hold values from 0 to 2
Outputs:
- lanczos_vector: float32 [4, 512, 512], P('narrow', 'wide')
- alpha: float32 [], replicated
The draws below stay inside these ranges and needn't reach their ends.
Inputs may be any that keep to these rules, and one draw needn't show every extreme that they name: `left_sizes`: basis states of each left sector; they add up to 1536, and some sector has exactly 512. `right_sizes`: basis states of each right sector; they add up to 1536, and some sector has exactly 512. `channel_charge`: 0 lowers the sector by one, 1 keeps it, 2 raises it by one.
All inputs are finite; a program needn't handle non-finite values.
Results may differ from the reference program's by a relative error of at most 0.0003.
Values sent between devices are 32-bit elements; how exact they have to be, the bound alone decides.
No kernel may reach another device: no remote copies, remote signals or barrier semaphores. Data moves between devices by JAX's collectives and lax.ppermute only.
A program may use at most 64 MiB of HBM per device.

```python
import math
import jax
import jax.numpy as jnp
import numpy as np
from jax import lax

W = 32
S = 512
K = 4
BOND = 1536


def draw_left_env(key, part):
    shape = (W, K, S, S)
    rowidx = lax.broadcasted_iota(jnp.int32, shape, 2)
    colidx = lax.broadcasted_iota(jnp.int32, shape, 3)
    diagonal = (rowidx == colidx).astype(jnp.float32)
    sub = jax.random.fold_in(key, 11)
    noise = jax.random.normal(sub, shape, jnp.float32)
    return noise * S ** (-0.5) + diagonal


def draw_right_env(key, part):
    shape = (W, K, S, S)
    rowidx = lax.broadcasted_iota(jnp.int32, shape, 2)
    colidx = lax.broadcasted_iota(jnp.int32, shape, 3)
    diagonal = (rowidx == colidx).astype(jnp.float32)
    sub = jax.random.fold_in(key, 23)
    noise = jax.random.normal(sub, shape, jnp.float32)
    return noise * S ** (-0.5) + diagonal


def set_ends(array, own_key, low, largest):
    longest = array.shape.index(max(array.shape))
    spots = []
    for shift in (0, 1):
        where = [jax.random.randint(jax.random.fold_in(own_key, axis), (), 0, length) for axis, length in enumerate(array.shape)]
        where[longest] = (where[longest] + shift) % array.shape[longest]
        spots.append(tuple(where))
    return array.at[spots[0]].set(low).at[spots[1]].set(largest)


def levels(rng, extent, cuts, smallest, top_value):
    level, own = 1.0, jax.random.fold_in(rng, 6)
    for axis_at, parts in cuts:
        heights = jnp.exp(jax.random.uniform(jax.random.fold_in(own, axis_at), (parts,), jnp.float32, smallest / len(cuts), top_value / len(cuts)))
        level = level * jnp.repeat(heights, extent[axis_at] // parts).reshape([-1 if axis == axis_at else 1 for axis in range(len(extent))])
    return level


def split_up(count, total, limit, skew):
    loads = [(1 << 20) // math.isqrt(rank ** skew) + 1 for rank in range(2, count + 1)]
    rest, holding = total - limit - (count - 1), [1] * (count - 1)
    while rest > 0:
        free = [i for i in range(count - 1) if holding[i] < limit]
        pool, left = sum([loads[i] for i in free]), rest
        for i in free:
            extra = min(limit - holding[i], max(1, left * loads[i] // pool), rest)
            holding[i] = holding[i] + extra
            rest = rest - extra
    return np.array([limit] + holding)


def ragged_sizes(own_key, count, total, bound, skew):
    if count == 2:
        one = jax.random.randint(own_key, (), max(1, total - bound), min(bound, total - 1) + 1)
        return jnp.stack([one, total - one])
    lengths = jnp.asarray(split_up(count, total, bound, skew), jnp.int32)
    pairs = (count - 1) // 2
    giver, receiver = lengths[1:1 + 2 * pairs:2], lengths[2:2 + 2 * pairs:2]
    room = jnp.minimum(giver - 1, bound - receiver)
    passed = jax.random.randint(jax.random.fold_in(own_key, 1), (pairs,), 0, 1 << 20) % (room + 1)
    lengths = lengths.at[1:1 + 2 * pairs:2].set(giver - passed).at[2:2 + 2 * pairs:2].set(receiver + passed)
    return lengths[jax.random.permutation(jax.random.fold_in(own_key, 2), count)]


def scatter_about(rng, extent, width, reach, pieces=(), kind=jnp.bfloat16):
    result = jax.random.normal(rng, extent, jnp.float32) * width
    if len(pieces) > 0:
        result = levels(rng, extent, pieces, -0.22, 0.18) * result
    return jnp.clip(result, min=-reach, max=reach).astype(kind)


def setup_inputs(seed: int = 0) -> dict:
    splits = jax.random.split(jax.random.key(seed), 7)
    state = scatter_about(splits[0], (K, S, S), 0.25, 1.5, ((0, 4),), jnp.float32)
    left_env = draw_left_env(jax.random.fold_in(splits[6], 71), 0)
    right_env = draw_right_env(jax.random.fold_in(splits[6], 71), 0)
    left_sizes = ragged_sizes(splits[3], K, BOND, S, 2).astype(jnp.int32)
    right_sizes = ragged_sizes(splits[4], K, BOND, S, 1).astype(jnp.int32)
    channel_charge = set_ends(jax.random.randint(splits[5], (W,), 0, 3), jax.random.fold_in(splits[5], 1), 0, 2).astype(jnp.int32)
    return {"state": state, "left_env": left_env, "right_env": right_env, "left_sizes": left_sizes, "right_sizes": right_sizes, "channel_charge": channel_charge}


def valid_table(sizes):
    positions = jnp.arange(S, dtype=jnp.int32)
    return (positions[None, :] < sizes[:, None]).astype(jnp.float32)


def reference(state, left_env, right_env, left_sizes, right_sizes, channel_charge):
    left_ok = valid_table(left_sizes)
    right_ok = valid_table(right_sizes)
    psi = state * left_ok[:, :, None] * right_ok[:, None, :]
    sectors = jnp.arange(K, dtype=jnp.int32)

    def one_channel(total, inputs):
        lenv, renv, charge = inputs
        source = sectors - (charge - 1)
        inside = ((source >= 0) & (source < K)).astype(jnp.float32)
        clipped = jnp.clip(source, 0, K - 1).astype(jnp.int32)
        psi_src = psi[clipped] * inside[:, None, None]
        left_src = left_ok[clipped] * inside[:, None]
        right_src = right_ok[clipped] * inside[:, None]
        lmat = lenv * left_ok[:, :, None] * left_src[:, None, :]
        rmat = renv * right_ok[:, :, None] * right_src[:, None, :]
        inner = jnp.einsum("kab,kbc->kac", lmat, psi_src, precision=lax.Precision.HIGHEST)
        term = jnp.einsum("kac,kdc->kad", inner, rmat, precision=lax.Precision.HIGHEST)
        return total + term, None

    hpsi, unused = lax.scan(one_channel, jnp.zeros((K, S, S), jnp.float32), (left_env, right_env, channel_charge))
    alpha = jnp.sum(psi * hpsi) / jnp.sum(psi * psi)
    return hpsi - alpha * psi, alpha
```

```python
import functools

import jax
import jax.numpy as jnp
from jax import lax
from jax.experimental import pallas as pl
from jax.experimental.pallas import tpu as pltpu
from jax.sharding import PartitionSpec as P

F32 = jnp.float32
BF16 = jnp.bfloat16
NN = (((1,), (0,)), ((), ()))
NT = (((1,), (1,)), ((), ()))
VMEM = pl.BlockSpec(memory_space=pltpu.VMEM)
SMEM = pl.BlockSpec(memory_space=pltpu.SMEM)
ANY = pl.BlockSpec(memory_space=pl.ANY)


def split(value):
    high = value.astype(BF16)
    low = (value - high.astype(F32)).astype(BF16)
    return high, low


def product(left, right, dims):
    (lh, ll), (rh, rl) = left, right
    dot = functools.partial(lax.dot_general, dimension_numbers=dims, preferred_element_type=F32)
    return dot(lh, rh) + (dot(lh, rl) + dot(ll, rh))


def size_at(sizes, sector):
    count = sizes.shape[0]
    inside = (sector >= 0) & (sector < count)
    return jnp.where(inside, sizes[jnp.clip(sector, 0, count - 1)], 0)


def keep(value, rows, cols, first_row=0):
    row = lax.broadcasted_iota(jnp.int32, value.shape, 0) + first_row
    col = lax.broadcasted_iota(jnp.int32, value.shape, 1)
    return jnp.where((row < rows) & (col < cols), value, 0.0)


def near_kernel(lsz, rsz, charge, own, near, left, right, total, lbuf, rbuf, psi_h, psi_l, sems):
    me = lax.axis_index("narrow")
    chans = left.shape[0]
    block = own.shape[0]
    partner = me + 1 - 2 * lax.rem(me, 2)

    def source(chan):
        return me - (charge[chan] - 1)

    def wanted(chan):
        src = source(chan)
        inside = (src >= 0) & (src < lsz.shape[0])
        return inside & ((src == me) | (src == partner))

    def copies(chan):
        return (
            pltpu.make_async_copy(right.at[chan, 0], rbuf.at[chan], sems.at[0, chan]),
            pltpu.make_async_copy(left.at[chan, 0], lbuf.at[chan], sems.at[1, chan]),
        )

    for chan in range(chans):

        @pl.when(wanted(chan))
        def _():
            for copy in copies(chan):
                copy.start()

    total[...] = jnp.zeros_like(total)
    for slot, (ref, sector) in enumerate(((own, me), (near, partner))):
        high, low = split(keep(ref[...], size_at(lsz, sector), size_at(rsz, sector)))
        psi_h[slot] = high
        psi_l[slot] = low

    def step(chan, carry):
        @pl.when(wanted(chan))
        def _():
            src = source(chan)
            slot = jnp.where(src == me, 0, 1)
            from_right, from_left = copies(chan)
            from_right.wait()
            rmat = split(keep(rbuf[chan], block, size_at(rsz, src)))
            y = split(product((psi_h[slot], psi_l[slot]), rmat, NT))
            from_left.wait()
            lmat = split(keep(lbuf[chan], block, size_at(lsz, src)))
            total[...] += product(lmat, y, NN)

        return carry

    lax.fori_loop(0, chans, step, 0)


def far_part(first, lsz, rsz, charge, far, left, right, total, lbuf, rbuf, sems):
    me = lax.axis_index("narrow")
    chans = left.shape[0]
    rows, block = far.shape
    other = me - 1 + 2 * lax.rem(me, 2)
    inside = (other >= 0) & (other < lsz.shape[0])

    def wanted(chan):
        return inside & (me - (charge[chan] - 1) == other)

    def copies(chan):
        return (
            pltpu.make_async_copy(right.at[chan, 0], rbuf.at[chan], sems.at[0, chan]),
            pltpu.make_async_copy(left.at[chan, 0, :, pl.ds(first, rows)], lbuf.at[chan], sems.at[1, chan]),
        )

    for chan in range(chans):

        @pl.when(wanted(chan))
        def _():
            for copy in copies(chan):
                copy.start()

    def step(chan, carry):
        @pl.when(wanted(chan))
        def _():
            lcount, rcount = size_at(lsz, other), size_at(rsz, other)
            psi = split(keep(far[...], lcount, rcount, first))
            from_right, from_left = copies(chan)
            from_right.wait()
            y = split(product(psi, split(keep(rbuf[chan], block, rcount)), NT))
            from_left.wait()
            lmat = split(keep(lbuf[chan], block, lcount - first))
            total[...] += product(lmat, y, NN)

        return carry

    lax.fori_loop(0, chans, step, 0)


def far_kernel(first, lsz, rsz, charge, far, left, right, before, total, lbuf, rbuf, sems):
    total[...] = before[...]
    far_part(first, lsz, rsz, charge, far, left, right, total, lbuf, rbuf, sems)


def last_kernel(first, lsz, rsz, charge, far, left, right, before, own, *rest):
    *outs, total, lbuf, rbuf, sems = rest
    total[...] = before[...]
    far_part(first, lsz, rsz, charge, far, left, right, total, lbuf, rbuf, sems)
    me = lax.axis_index("narrow")
    rows, cols = size_at(lsz, me), size_at(rsz, me)
    hpsi = keep(total[...], rows, cols)
    total[...] = hpsi
    numerator = jnp.sum(keep(own[...], rows, cols) * hpsi)
    here = lax.axis_index("wide")
    block = own.shape[0]
    band = block // len(outs)
    for shift, out in enumerate(outs):
        start = pl.multiple_of((here ^ shift) * band, band)
        out[:band, :] = total[pl.ds(start, band), :]
        out[band:, :] = jnp.full((out.shape[0] - band, out.shape[1]), numerator, F32)


def gather_kernel(lsz, rsz, own, *rest):
    *parts, share, sums = rest
    band = share.shape[0]
    whole = parts[0][...]
    for part in parts[1:]:
        whole += part[...]
    share[...] = whole[:band]
    me = lax.axis_index("narrow")
    psi = keep(own[...], size_at(lsz, me), size_at(rsz, me))
    denominator = jnp.sum(psi * psi)
    row = lax.broadcasted_iota(jnp.int32, sums.shape, 0)
    sums[...] = jnp.where(row == 0, whole[band : band + 8, : sums.shape[1]], denominator)


def final_kernel(lsz, rsz, own, share, *rest):
    *sums, out, alpha = rest
    both = sums[0][...]
    for more in sums[1:]:
        both += more[...]
    ratio = both[0:1, :] / both[1:2, :]
    me = lax.axis_index("narrow")
    band = share.shape[0]
    start = pl.multiple_of(lax.axis_index("wide") * band, band)
    psi = keep(own[pl.ds(start, band), :], size_at(lsz, me), size_at(rsz, me), start)
    out[...] = share[...] - jnp.concatenate([ratio] * (psi.shape[1] // ratio.shape[1]), axis=1) * psi
    alpha[...] = ratio


def exchange(value, axis, shift):
    count = lax.axis_size(axis)
    return lax.ppermute(value, axis, [(i, i ^ shift) for i in range(count)])


def per_device(state, left_env, right_env, left_sizes, right_sizes, channel_charge):
    chans, _, block, _ = left_env.shape
    n_wide, n_narrow = lax.axis_size("wide"), lax.axis_size("narrow")
    band = block // n_wide
    own = state[0]
    params = pltpu.CompilerParams(vmem_limit_bytes=40 * 2**20)
    scalars = (left_sizes, right_sizes, channel_charge)
    square = jax.ShapeDtypeStruct((block, block), F32)

    ends = [(0, 0), (n_narrow - 1, n_narrow - 1)]
    across = [pair for k in range(1, n_narrow - 1, 2) for pair in ((k, k + 1), (k + 1, k))]
    near = exchange(own, "narrow", 1)
    chunks = 2
    rows = block // chunks
    fars = [lax.ppermute(own[i * rows : (i + 1) * rows], "narrow", across + ends) for i in range(chunks)]

    total = pl.pallas_call(
        near_kernel,
        out_shape=square,
        in_specs=[SMEM] * 3 + [VMEM] * 2 + [ANY] * 2,
        out_specs=VMEM,
        scratch_shapes=[
            pltpu.VMEM((chans, block, block), F32),
            pltpu.VMEM((chans, block, block), F32),
            pltpu.VMEM((2, block, block), BF16),
            pltpu.VMEM((2, block, block), BF16),
            pltpu.SemaphoreType.DMA((2, chans)),
        ],
        compiler_params=params,
        name="near",
    )(*scalars, own, near, left_env, right_env)

    far_scratch = [
        pltpu.VMEM((chans, block, rows), F32),
        pltpu.VMEM((chans, block, block), F32),
        pltpu.SemaphoreType.DMA((2, chans)),
    ]
    for i in range(chunks - 1):
        total = pl.pallas_call(
            functools.partial(far_kernel, i * rows),
            out_shape=square,
            in_specs=[SMEM] * 3 + [VMEM] + [ANY] * 2 + [VMEM],
            out_specs=VMEM,
            scratch_shapes=far_scratch,
            compiler_params=params,
            name="far",
        )(*scalars, fars[i], left_env, right_env, total)
    message = jax.ShapeDtypeStruct((band + 8, block), F32)
    bands = pl.pallas_call(
        functools.partial(last_kernel, (chunks - 1) * rows),
        out_shape=[message] * n_wide,
        in_specs=[SMEM] * 3 + [VMEM] + [ANY] * 2 + [VMEM] * 2,
        out_specs=[VMEM] * n_wide,
        scratch_shapes=[pltpu.VMEM((block, block), F32)] + far_scratch,
        compiler_params=params,
        name="last",
    )(*scalars, fars[-1], left_env, right_env, total, own)

    parts = [bands[0]] + [exchange(bands[s], "wide", s) for s in range(n_wide - 1, 0, -1)]
    small = jax.ShapeDtypeStruct((8, 128), F32)
    share, sums = pl.pallas_call(
        gather_kernel,
        out_shape=[jax.ShapeDtypeStruct((band, block), F32), small],
        in_specs=[SMEM] * 2 + [VMEM] * (1 + n_wide),
        out_specs=[VMEM, VMEM],
        compiler_params=params,
        name="gather",
    )(left_sizes, right_sizes, own, *parts)
    every = [sums] + [exchange(sums, "narrow", s) for s in range(1, n_narrow)]
    out, alpha = pl.pallas_call(
        final_kernel,
        out_shape=[jax.ShapeDtypeStruct((band, block), F32), jax.ShapeDtypeStruct((1, 128), F32)],
        in_specs=[SMEM] * 2 + [VMEM] * (2 + len(every)),
        out_specs=[VMEM, VMEM],
        compiler_params=params,
        name="final",
    )(left_sizes, right_sizes, own, share, *every)
    return out[None], alpha[0, 0]


def solution(mesh):
    placed = (
        P("narrow", None, None),
        P("wide", "narrow", None, None),
        P("wide", "narrow", None, None),
        P(),
        P(),
        P("wide"),
    )
    return jax.shard_map(
        per_device,
        mesh=mesh,
        in_specs=placed,
        out_specs=(P("narrow", "wide", None), P()),
        check_vma=False,
    )
```

```python
import functools

import jax
import jax.numpy as jnp
from jax import lax
from jax.experimental import pallas as pl
from jax.experimental.pallas import tpu as pltpu
from jax.sharding import PartitionSpec as P

F32 = jnp.float32
BF16 = jnp.bfloat16
NN = (((1,), (0,)), ((), ()))
NT = (((1,), (1,)), ((), ()))
VMEM = pl.BlockSpec(memory_space=pltpu.VMEM)
HBM = pl.BlockSpec(memory_space=pltpu.HBM)
FAR_ROWS = (1, 1)
OWN, NEAR, FAR = 0, 1, 2
TAIL = 8


def split(value):
    high = value.astype(BF16)
    low = (value - high.astype(F32)).astype(BF16)
    return high, low


def product(left, right, dims):
    (lh, ll), (rh, rl) = left, right
    dot = functools.partial(lax.dot_general, dimension_numbers=dims, preferred_element_type=F32)
    return dot(lh, rh) + (dot(lh, rl) + dot(ll, rh))


def keep(value, rows, cols, first_row=0):
    col = lax.broadcasted_iota(jnp.int32, value.shape, 1)
    if rows is None:
        return jnp.where(col < cols, value, 0.0)
    row = lax.broadcasted_iota(jnp.int32, value.shape, 0) + first_row
    return jnp.where((row < rows) & (col < cols), value, 0.0)


def add_channels(kind, first, table, psi_ref, lh, ll, rh, rl, total, ph, pl_):
    rows = psi_ref.shape[0]
    chans = lh.shape[0]
    have = table[0, 6 + kind]
    listed = [table[0, 9 + kind * chans + i] for i in range(chans)]

    def channel(at):
        found = listed[0]
        for i in range(1, chans):
            found = jnp.where(at == i, listed[i], found)
        return found

    @pl.when(have > 0)
    def _():
        ph[:rows], pl_[:rows] = split(keep(psi_ref[...], table[0, 2 * kind], table[0, 2 * kind + 1], first))

        def group(start, size):
            ids = [channel(start + i) for i in range(size)]
            psi = (ph[:rows], pl_[:rows])
            ys = [split(product(psi, (rh[c], rl[c]), NT)) for c in ids]
            more = None
            for c, y in zip(ids, ys):
                lmat = (lh[c, :, pl.ds(first, rows)], ll[c, :, pl.ds(first, rows)])
                term = product(lmat, y, NN)
                more = term if more is None else more + term
            total[...] += more

        def pairs(i, carry):
            group(2 * i, 2)
            return carry

        if chans > 1:
            lax.fori_loop(0, have // 2, pairs, 0)

        @pl.when(lax.rem(have, 2) == 1)
        def _():
            group(have - 1, 1)


def prep_kernel(
    lsz, rsz, charge, state, left, right,
    table, psi, psi_band, norm, lh, ll, rh, rl,
    ls, rs, cs, lbuf, rbuf, sbuf, sems, more,
):
    chans = left.shape[0]
    me = lax.axis_index("narrow")
    count = ls.shape[0]
    small = [
        pltpu.make_async_copy(src, dst, more.at[i])
        for i, (src, dst) in enumerate(((lsz, ls), (rsz, rs), (charge, cs)))
    ]
    rights = [pltpu.make_async_copy(right.at[c, 0], rbuf.at[c], sems.at[0, c]) for c in range(chans)]
    lefts = [pltpu.make_async_copy(left.at[c, 0], lbuf.at[c], sems.at[1, c]) for c in range(chans)]
    whole = pltpu.make_async_copy(state.at[0], sbuf, more.at[3])
    for copy in small:
        copy.start()
    for c in range(chans):
        rights[c].start()
        lefts[c].start()
    whole.start()
    for copy in small:
        copy.wait()

    side = 1 - 2 * lax.rem(me, 2)
    sectors = (me, me + side, me - side)

    def size_at(sizes, sector):
        inside = (sector >= 0) & (sector < count)
        return jnp.where(inside, sizes[jnp.clip(sector, 0, count - 1)], 0)

    place = lax.broadcasted_iota(jnp.int32, table.shape, 1)
    entries = jnp.zeros(table.shape, jnp.int32)
    for kind, sector in enumerate(sectors):
        entries = jnp.where(place == 2 * kind, size_at(ls, sector), entries)
        entries = jnp.where(place == 2 * kind + 1, size_at(rs, sector), entries)
        have = 0
        for c in range(chans):
            src = me - (cs[c] - 1)
            match = (src == sector) & (sector >= 0) & (sector < count)
            entries = jnp.where(match & (place == 9 + kind * chans + have), c, entries)
            have += match.astype(jnp.int32)
        entries = jnp.where(place == 6 + kind, have, entries)
    table[...] = entries

    for c in range(chans):
        src = me - (cs[c] - 1)
        rights[c].wait()
        rh[c], rl[c] = split(keep(rbuf[c], None, size_at(rs, src)))
        lefts[c].wait()
        lh[c], ll[c] = split(keep(lbuf[c], None, size_at(ls, src)))

    whole.wait()
    masked = keep(sbuf[...], size_at(ls, me), size_at(rs, me))
    psi[...] = masked
    norm[...] = jnp.full(norm.shape, jnp.sum(masked * masked), F32)
    band = psi_band.shape[0]
    psi_band[...] = psi[pl.ds(pl.multiple_of(lax.axis_index("wide") * band, band), band), :]


def near_kernel(table, near, psi, lh, ll, rh, rl, total, ph, pl_):
    total[...] = jnp.zeros_like(total)
    add_channels(OWN, 0, table, psi, lh, ll, rh, rl, total, ph, pl_)
    add_channels(NEAR, 0, table, near, lh, ll, rh, rl, total, ph, pl_)


def far_kernel(first, table, psi_ref, lh, ll, rh, rl, before, total, ph, pl_):
    add_channels(FAR, first, table, psi_ref, lh, ll, rh, rl, total, ph, pl_)


def last_kernel(first, orders, table, psi_ref, lh, ll, rh, rl, before, psi, norm, *rest):
    *outs, total, ph, pl_ = rest
    total[...] = before[...]
    add_channels(FAR, first, table, psi_ref, lh, ll, rh, rl, total, ph, pl_)
    hpsi = keep(total[...], table[0, 0], table[0, 1])
    total[...] = hpsi
    numerator = jnp.sum(psi[...] * hpsi)
    here = lax.axis_index("wide")
    band = psi.shape[0] // lax.axis_size("wide")
    row = lax.broadcasted_iota(jnp.int32, (TAIL, psi.shape[1]), 0)
    sums = jnp.where(row == 0, numerator, norm[0, 0])
    for order, out in zip(orders, outs):
        for place, shift in enumerate(order):
            start = pl.multiple_of((here ^ shift) * band, band)
            out[place * band : (place + 1) * band, :] = total[pl.ds(start, band), :]
        if out.shape[0] > len(order) * band:
            out[len(order) * band :, :] = sums


def add_up(parts):
    parts = [part[...] for part in parts]
    whole = parts[0]
    for part in parts[1:]:
        whole += part
    tail = jnp.concatenate([whole[-TAIL : 1 - TAIL], parts[0][1 - TAIL :]], axis=0)
    return whole[:-TAIL], tail


def merge_kernel(*refs):
    *parts, mine, give = refs
    whole, sums = add_up(parts)
    half = mine.shape[0] - TAIL
    mine[:half, :] = whole[:half]
    give[:half, :] = whole[half:]
    mine[half:, :] = sums
    give[half:, :] = sums


def pass_kernel(*refs):
    *parts, out = refs
    whole, sums = add_up(parts)
    out[:-TAIL, :] = whole
    out[-TAIL:, :] = sums


def gather_kernel(n_plain, *refs):
    *parts, share, sums = refs
    whole, tail = add_up(parts[n_plain:])
    for part in parts[:n_plain]:
        whole += part[...]
    share[...] = whole
    sums[...] = tail[:, : sums.shape[1]]


def final_kernel(psi, share, *rest):
    *sums, out, alpha = rest
    both = sums[0][...]
    for more in sums[1:]:
        both += more[...]
    ratio = both[0:1, :] / both[1:2, :]
    out[...] = share[...] - jnp.concatenate([ratio] * (psi.shape[1] // ratio.shape[1]), axis=1) * psi[...]
    alpha[...] = ratio


def exchange(value, axis, shift):
    count = lax.axis_size(axis)
    return lax.ppermute(value, axis, [(i, i ^ shift) for i in range(count)])


def f32(*shape):
    return jax.ShapeDtypeStruct(shape, F32)


def call(kernel, out_shape, n_in, out_specs, scratch=(), limit=16, name=None, **more):
    return pl.pallas_call(
        kernel,
        out_shape=out_shape,
        in_specs=[VMEM] * n_in,
        out_specs=out_specs,
        scratch_shapes=scratch,
        compiler_params=pltpu.CompilerParams(vmem_limit_bytes=limit * 2**20),
        name=name,
        **more,
    )


def per_device(state, left_env, right_env, left_sizes, right_sizes, channel_charge):
    chans, _, block, _ = left_env.shape
    n_wide, n_narrow = lax.axis_size("wide"), lax.axis_size("narrow")
    band = block // n_wide
    own = state[0]

    ends = [(0, 0), (n_narrow - 1, n_narrow - 1)]
    across = [pair for k in range(1, n_narrow - 1, 2) for pair in ((k, k + 1), (k + 1, k))]
    cuts = [0]
    for share in FAR_ROWS:
        cuts.append(cuts[-1] + share * block // sum(FAR_ROWS))
    fars = [lax.ppermute(own[a:b], "narrow", across + ends) for a, b in zip(cuts, cuts[1:])]
    near = exchange(own, "narrow", 1)

    halves = jax.ShapeDtypeStruct((chans, block, block), BF16)
    table, psi, psi_band, norm, *envs = pl.pallas_call(
        prep_kernel,
        out_shape=[jax.ShapeDtypeStruct((8, 128), jnp.int32), f32(block, block), f32(band, block), f32(8, 128)]
        + [halves] * 4,
        in_specs=[HBM] * 6,
        out_specs=[VMEM] * 8,
        scratch_shapes=[
            pltpu.SMEM(left_sizes.shape, jnp.int32),
            pltpu.SMEM(right_sizes.shape, jnp.int32),
            pltpu.SMEM(channel_charge.shape, jnp.int32),
            pltpu.VMEM((chans, block, block), F32),
            pltpu.VMEM((chans, block, block), F32),
            pltpu.VMEM((block, block), F32),
            pltpu.SemaphoreType.DMA((2, chans)),
            pltpu.SemaphoreType.DMA((4,)),
        ],
        compiler_params=pltpu.CompilerParams(vmem_limit_bytes=32 * 2**20),
        name="prep",
    )(
        left_sizes, right_sizes, channel_charge,
        *(pltpu.with_memory_space_constraint(x, pltpu.HBM) for x in (state, left_env, right_env)),
    )

    square = f32(block, block)
    pair = [pltpu.VMEM((block, block), BF16)] * 2
    total = call(near_kernel, square, 7, VMEM, pair, name="near")(table, near, psi, *envs)
    for first, far in zip(cuts[:-2], fars[:-1]):
        total = call(
            functools.partial(far_kernel, first), square, 7, VMEM, pair, name="far", input_output_aliases={6: 0}
        )(table, far, *envs, total)

    def last(orders, shapes):
        return call(
            functools.partial(last_kernel, cuts[-2], orders),
            [f32(rows, block) for rows in shapes], 9, [VMEM] * len(orders),
            [pltpu.VMEM((block, block), F32)] + pair, name="last",
        )(table, fars[-1], *envs, total, psi, norm)

    groups = min(4, n_wide)
    held = n_wide // groups
    orders = [[s + groups * place for place in range(held)] for s in range(groups)]
    blocks = last(orders, [held * band + TAIL] * groups)
    plain = []
    parts = [blocks[0]] + [exchange(blocks[s], "wide", s) for s in range(groups - 1, 0, -1)]
    while held > 1:
        held //= 2
        mine, give = call(merge_kernel, [f32(held * band + TAIL, block)] * 2, len(parts), [VMEM] * 2, name="merge")(
            *parts
        )
        parts = [mine, exchange(give, "wide", groups * held)]

    share, sums = call(
        functools.partial(gather_kernel, len(plain)), [f32(band, block), f32(8, 128)], len(plain) + len(parts),
        [VMEM] * 2, name="gather",
    )(*plain, *parts)
    every = [sums] + [exchange(sums, "narrow", s) for s in range(1, n_narrow)]
    out, alpha = call(final_kernel, [f32(band, block), f32(1, 128)], 2 + len(every), [VMEM] * 2, name="final")(
        psi_band, share, *every
    )
    return out[None], alpha[0, 0]


def solution(mesh):
    placed = (
        P("narrow", None, None),
        P("wide", "narrow", None, None),
        P("wide", "narrow", None, None),
        P(),
        P(),
        P("wide"),
    )
    return jax.shard_map(
        per_device,
        mesh=mesh,
        in_specs=placed,
        out_specs=(P("narrow", "wide", None), P()),
        check_vma=False,
    )
```

```python
import functools

import jax
import jax.numpy as jnp
from jax import lax
from jax.experimental import pallas as pl
from jax.experimental.pallas import tpu as pltpu
from jax.sharding import PartitionSpec as P

F32 = jnp.float32
BF16 = jnp.bfloat16
NN = (((1,), (0,)), ((), ()))
NT = (((1,), (1,)), ((), ()))
VMEM = pl.BlockSpec(memory_space=pltpu.VMEM)
HBM = pl.BlockSpec(memory_space=pltpu.HBM)
OWN, NEAR, FAR, NONE = range(4)


def split(value):
    high = value.astype(BF16)
    low = (value - high.astype(F32)).astype(BF16)
    return high, low


def product(left, right, dims):
    (lh, ll), (rh, rl) = left, right
    dot = functools.partial(lax.dot_general, dimension_numbers=dims, preferred_element_type=F32)
    return dot(lh, rh) + (dot(lh, rl) + dot(ll, rh))


def keep(value, rows, cols, first_row=0):
    row = lax.broadcasted_iota(jnp.int32, value.shape, 0) + first_row
    col = lax.broadcasted_iota(jnp.int32, value.shape, 1)
    return jnp.where((row < rows) & (col < cols), value, 0.0)


def band_order(n_wide):
    groups = min(4, n_wide)
    return [s + groups * t for s in range(groups) for t in range(n_wide // groups)]


def main_kernel(
    lsz, rsz, charge, state, left, right, near,
    table, psi, psi_band, norm, lh, ll, rh, rl, total,
    ls, rs, cs, lbuf, rbuf, sbuf, ph, pl_, sems, more,
):
    chans, block = left.shape[0], state.shape[1]
    me, here = lax.axis_index("narrow"), lax.axis_index("wide")
    count = ls.shape[0]
    small = [
        pltpu.make_async_copy(src, dst, more.at[i])
        for i, (src, dst) in enumerate(((lsz, ls), (rsz, rs), (charge, cs)))
    ]
    whole = pltpu.make_async_copy(state.at[0], sbuf, more.at[3])
    for copy in small + [whole]:
        copy.start()
    for copy in small:
        copy.wait()

    side = 1 - 2 * lax.rem(me, 2)
    sectors = (me, me + side, me - side)

    def size_at(sizes, sector):
        inside = (sector >= 0) & (sector < count)
        return jnp.where(inside, sizes[jnp.clip(sector, 0, count - 1)], 0)

    lcounts = [size_at(ls, sector) for sector in sectors] + [0]
    rcounts = [size_at(rs, sector) for sector in sectors] + [0]

    def pick(values, kind):
        found = values[NONE]
        for i in (OWN, NEAR, FAR):
            found = jnp.where(kind == i, values[i], found)
        return found

    kinds = []
    for c in range(chans):
        src = me - (cs[c] - 1)
        kind = jnp.where(src == me, OWN, jnp.where(src == sectors[NEAR], NEAR, FAR))
        kinds.append(jnp.where((src >= 0) & (src < count), kind, NONE))
    places = [
        sum((kinds[o] < kinds[c]).astype(jnp.int32) for o in range(chans))
        + sum((kinds[o] == kinds[c]).astype(jnp.int32) for o in range(c))
        for c in range(chans)
    ]
    copies = []
    for j in range(chans):
        chan = sum(jnp.where(places[c] == j, c, 0) for c in range(chans))
        copies.append(
            (
                pltpu.make_async_copy(right.at[chan, 0], rbuf.at[j], sems.at[0, j]),
                pltpu.make_async_copy(left.at[chan, 0], lbuf.at[j], sems.at[1, j]),
            )
        )
        for copy in copies[-1]:
            copy.start()

    n_close = sum((k <= NEAR).astype(jnp.int32) for k in kinds)
    n_far = sum((k == FAR).astype(jnp.int32) for k in kinds)
    place = lax.broadcasted_iota(jnp.int32, table.shape, 1)
    entries = jnp.where(place == 0, lcounts[FAR], jnp.where(place == 1, rcounts[FAR], 0))
    table[...] = jnp.where(place == 2, n_close, jnp.where(place == 3, n_close + n_far, entries))

    order = band_order(lax.axis_size("wide"))
    band = psi_band.shape[0]
    starts = [pl.multiple_of((here ^ shift) * band, band) for shift in order]

    total[...] = jnp.zeros_like(total)
    ph[NEAR], pl_[NEAR] = split(keep(near[...], lcounts[NEAR], rcounts[NEAR]))
    whole.wait()
    masked = keep(sbuf[...], lcounts[OWN], rcounts[OWN])
    ph[OWN], pl_[OWN] = split(masked)
    norm[...] = jnp.full(norm.shape, jnp.sum(masked * masked), F32)
    sbuf[...] = masked
    psi_band[...] = sbuf[pl.ds(pl.multiple_of(here * band, band), band), :]
    for p, start in enumerate(starts):
        psi[p * band : (p + 1) * band, :] = sbuf[pl.ds(start, band), :]

    for j in range(chans):
        kind = sum(jnp.where(places[c] == j, kinds[c], 0) for c in range(chans))
        lcount, rcount = pick(lcounts, kind), pick(rcounts, kind)
        for copy in copies[j]:
            copy.wait()

        def halve():
            rh[j], rl[j] = split(keep(rbuf[j], rcounts[OWN], rcount))
            for p, start in enumerate(starts):
                rows = slice(p * band, (p + 1) * band)
                piece = keep(lbuf[j, pl.ds(start, band), :], lcounts[OWN], lcount, start)
                lh[j, rows, :], ll[j, rows, :] = split(piece)

        @pl.when(kind <= NEAR)
        def _():
            halve()
            y = split(product((ph[kind], pl_[kind]), (rh[j], rl[j]), NT))
            total[...] += product((lh[j], ll[j]), y, NN)

        @pl.when(kind > NEAR)
        def _():
            halve()


def over_far(table, chans, group):
    first, have = table[0, 2], table[0, 3] - table[0, 2]
    for count in range(1, chans + 1):

        @pl.when(have == count)
        def _():
            group([first + i for i in range(count)])


def far_kernel(table, far, lh, ll, rh, rl, before, total, ph, pl_):
    rows = far.shape[0]

    @pl.when(table[0, 3] > table[0, 2])
    def _():
        ph[...], pl_[...] = split(keep(far[...], table[0, 0], table[0, 1]))

        def group(slots):
            psi = (ph[...], pl_[...])
            ys = [split(product(psi, (rh[j], rl[j]), NT)) for j in slots]
            terms = [product((lh[j, :, :rows], ll[j, :, :rows]), y, NN) for j, y in zip(slots, ys)]
            total[...] += functools.reduce(jnp.add, terms)

        over_far(table, lh.shape[0], group)


def last_kernel(table, far, lh, ll, rh, rl, before, psi, norm, sums, *rest):
    *outs, total, ph, pl_ = rest
    rows = far.shape[0]
    block = psi.shape[0]
    total[...] = before[...]

    @pl.when(table[0, 3] > table[0, 2])
    def _():
        ph[...], pl_[...] = split(keep(far[...], table[0, 0], table[0, 1], block - rows))

        def group(slots):
            psi_far = (ph[...], pl_[...])
            ys = [split(product(psi_far, (rh[j], rl[j]), NT)) for j in slots]
            terms = [
                product((lh[j, :, block - rows :], ll[j, :, block - rows :]), y, NN) for j, y in zip(slots, ys)
            ]
            total[...] += functools.reduce(jnp.add, terms)

        over_far(table, lh.shape[0], group)

    row = lax.broadcasted_iota(jnp.int32, sums.shape, 0)
    sums[...] = jnp.where(row == 0, jnp.sum(psi[...] * total[...]), norm[...])
    size = outs[0].shape[0]
    for i, out in enumerate(outs):
        out[...] = total[i * size : (i + 1) * size, :]


def add_kernel(*refs):
    *parts, out = refs
    whole = parts[0][...]
    for part in parts[1:]:
        whole += part[...]
    out[...] = whole


def add_first_kernel(*refs):
    *parts, out = refs
    whole = parts[0][...]
    for part in parts[1:]:
        whole += part[...]
    row = lax.broadcasted_iota(jnp.int32, out.shape, 0)
    out[...] = jnp.where(row == 0, whole, parts[0][...])


def merge_kernel(_, *refs):
    *parts, mine, give = refs
    whole = parts[0][...]
    for part in parts[1:]:
        whole += part[...]
    half = mine.shape[0]
    mine[...] = whole[:half]
    give[...] = whole[half:]


def final_kernel(n_parts, psi, *rest):
    parts, (*sums, out, alpha) = rest[:n_parts], rest[n_parts:]
    numerator = sums[0][0:1, :]
    for more in sums[1:]:
        numerator += more[0:1, :]
    ratio = numerator / sums[0][1:2, :]
    share = parts[0][...]
    for part in parts[1:]:
        share += part[...]
    out[...] = share - jnp.concatenate([ratio] * (psi.shape[1] // ratio.shape[1]), axis=1) * psi[...]
    alpha[...] = ratio


def exchange(value, axis, shift):
    count = lax.axis_size(axis)
    return lax.ppermute(value, axis, [(i, i ^ shift) for i in range(count)])


def f32(*shape):
    return jax.ShapeDtypeStruct(shape, F32)


def cost(flops, size=2**20):
    return pl.CostEstimate(flops=flops, bytes_accessed=size, transcendentals=0)


def call(kernel, out_shape, n_in, scratch=(), name=None, **more):
    return pl.pallas_call(
        kernel,
        out_shape=out_shape,
        in_specs=[VMEM] * n_in,
        out_specs=jax.tree.map(lambda _: VMEM, out_shape),
        scratch_shapes=scratch,
        compiler_params=pltpu.CompilerParams(vmem_limit_bytes=16 * 2**20),
        name=name,
        **more,
    )


def per_device(state, left_env, right_env, left_sizes, right_sizes, channel_charge):
    chans, _, block, _ = left_env.shape
    n_wide, n_narrow = lax.axis_size("wide"), lax.axis_size("narrow")
    band, half = block // n_wide, block // 2
    own = state[0]
    square, small = f32(block, block), f32(8, 128)
    work = 6 * chans * block**3

    ends = [(0, 0), (n_narrow - 1, n_narrow - 1)]
    across = [pair for k in range(1, n_narrow - 1, 2) for pair in ((k, k + 1), (k + 1, k))]
    far_top, far_low = (lax.ppermute(rows, "narrow", across + ends) for rows in (own[:half], own[half:]))
    near = exchange(own, "narrow", 1)

    halves = jax.ShapeDtypeStruct((chans, block, block), BF16)
    table, psi, psi_band, norm, lh, ll, rh, rl, total = pl.pallas_call(
        main_kernel,
        out_shape=[jax.ShapeDtypeStruct((8, 128), jnp.int32), square, f32(band, block), small]
        + [halves] * 4
        + [square],
        in_specs=[HBM] * 6 + [VMEM],
        out_specs=[VMEM] * 9,
        scratch_shapes=[
            pltpu.SMEM(left_sizes.shape, jnp.int32),
            pltpu.SMEM(right_sizes.shape, jnp.int32),
            pltpu.SMEM(channel_charge.shape, jnp.int32),
            pltpu.VMEM((chans, block, block), F32),
            pltpu.VMEM((chans, block, block), F32),
            pltpu.VMEM((block, block), F32),
            pltpu.VMEM((2, block, block), BF16),
            pltpu.VMEM((2, block, block), BF16),
            pltpu.SemaphoreType.DMA((2, chans)),
            pltpu.SemaphoreType.DMA((4,)),
        ],
        compiler_params=pltpu.CompilerParams(vmem_limit_bytes=32 * 2**20),
        cost_estimate=cost(work, 8 * chans * block * block),
        name="main",
    )(
        left_sizes, right_sizes, channel_charge,
        *(pltpu.with_memory_space_constraint(x, pltpu.HBM) for x in (state, left_env, right_env)),
        near,
    )
    envs = (lh, ll, rh, rl)

    pair = [pltpu.VMEM((half, block), BF16)] * 2
    total = call(far_kernel, square, 7, pair, name="far", cost_estimate=cost(work), input_output_aliases={6: 0})(table, far_top, *envs, total)

    groups = min(4, n_wide)
    held = n_wide // groups
    sums, *blocks = call(
        last_kernel, [small] + [f32(held * band, block)] * groups, 9, [pltpu.VMEM((block, block), F32)] + pair,
        name="last", cost_estimate=cost(work),
    )(table, far_low, *envs, total, psi, norm)
    parts = [blocks[0]] + [exchange(blocks[s], "wide", s) for s in range(groups - 1, 0, -1)]

    if n_narrow <= 4:
        every = [exchange(sums, "narrow", s) for s in range(n_narrow - 1, 0, -1)]
        sums = call(add_kernel, small, n_narrow, name="sectors")(sums, *every)
    else:
        step = 1
        while step < n_narrow:
            sums = call(add_kernel, small, 2, name="sectors")(sums, exchange(sums, "narrow", step))
            step *= 2
    sums = call(add_first_kernel, small, 2, name="pair")(sums, exchange(sums, "wide", 1))
    others = [exchange(sums, "wide", s) for s in range(n_wide - 2, 0, -2)]
    while held > 1:
        held //= 2
        mine, give = call(merge_kernel, [f32(held * band, block)] * 2, 1 + len(parts), name="merge")(sums, *parts)
        parts = [mine, exchange(give, "wide", groups * held)]

    out, alpha = call(
        functools.partial(final_kernel, len(parts)), [f32(band, block), f32(1, 128)], 2 + len(parts) + len(others),
        name="final",
    )(psi_band, *parts, sums, *others)
    return out[None], alpha[0, 0]


def solution(mesh):
    placed = (
        P("narrow", None, None),
        P("wide", "narrow", None, None),
        P("wide", "narrow", None, None),
        P(),
        P(),
        P("wide"),
    )
    return jax.shard_map(
        per_device,
        mesh=mesh,
        in_specs=placed,
        out_specs=(P("narrow", "wide", None), P()),
        check_vma=False,
    )
```

```python
import functools

import jax
import jax.numpy as jnp
from jax import lax
from jax.experimental import pallas as pl
from jax.experimental.pallas import tpu as pltpu
from jax.sharding import PartitionSpec as P

F32 = jnp.float32
BF16 = jnp.bfloat16
NN = (((1,), (0,)), ((), ()))
NT = (((1,), (1,)), ((), ()))
VMEM = pl.BlockSpec(memory_space=pltpu.VMEM)
HBM = pl.BlockSpec(memory_space=pltpu.HBM)
OWN, NEAR, FAR, NONE = range(4)
TAIL = 8


def split(value):
    high = value.astype(BF16)
    low = (value - high.astype(F32)).astype(BF16)
    return high, low


def product(left, right, dims):
    (lh, ll), (rh, rl) = left, right
    dot = functools.partial(lax.dot_general, dimension_numbers=dims, preferred_element_type=F32)
    return dot(lh, rh) + (dot(lh, rl) + dot(ll, rh))


def keep(value, rows, cols, first_row=0):
    row = lax.broadcasted_iota(jnp.int32, value.shape, 0) + first_row
    col = lax.broadcasted_iota(jnp.int32, value.shape, 1)
    return jnp.where((row < rows) & (col < cols), value, 0.0)


def band_order(n_wide):
    groups = min(4, n_wide)
    return [s + groups * t for s in range(groups) for t in range(n_wide // groups)]


def main_kernel(
    lsz, rsz, charge, state, left, right, near,
    table, psi, psi_band, norm, lh, ll, rh, rl, total,
    ls, rs, cs, lbuf, rbuf, sbuf, ph, pl_, sems, more,
):
    chans, block = left.shape[0], state.shape[1]
    me, here = lax.axis_index("narrow"), lax.axis_index("wide")
    count = ls.shape[0]
    small = [
        pltpu.make_async_copy(src, dst, more.at[i])
        for i, (src, dst) in enumerate(((lsz, ls), (rsz, rs), (charge, cs)))
    ]
    whole = pltpu.make_async_copy(state.at[0], sbuf, more.at[3])
    for copy in small + [whole]:
        copy.start()
    for copy in small:
        copy.wait()

    side = 1 - 2 * lax.rem(me, 2)
    sectors = (me, me + side, me - side)

    def size_at(sizes, sector):
        inside = (sector >= 0) & (sector < count)
        return jnp.where(inside, sizes[jnp.clip(sector, 0, count - 1)], 0)

    lcounts = [size_at(ls, sector) for sector in sectors] + [0]
    rcounts = [size_at(rs, sector) for sector in sectors] + [0]

    def pick(values, kind):
        found = values[NONE]
        for i in (OWN, NEAR, FAR):
            found = jnp.where(kind == i, values[i], found)
        return found

    kinds = []
    for c in range(chans):
        src = me - (cs[c] - 1)
        kind = jnp.where(src == me, OWN, jnp.where(src == sectors[NEAR], NEAR, FAR))
        kinds.append(jnp.where((src >= 0) & (src < count), kind, NONE))
    places = [
        sum((kinds[o] < kinds[c]).astype(jnp.int32) for o in range(chans))
        + sum((kinds[o] == kinds[c]).astype(jnp.int32) for o in range(c))
        for c in range(chans)
    ]
    copies = []
    for j in range(chans):
        chan = sum(jnp.where(places[c] == j, c, 0) for c in range(chans))
        copies.append(
            (
                pltpu.make_async_copy(right.at[chan, 0], rbuf.at[j], sems.at[0, j]),
                pltpu.make_async_copy(left.at[chan, 0], lbuf.at[j], sems.at[1, j]),
            )
        )
        for copy in copies[-1]:
            copy.start()

    n_close = sum((k <= NEAR).astype(jnp.int32) for k in kinds)
    n_far = sum((k == FAR).astype(jnp.int32) for k in kinds)
    place = lax.broadcasted_iota(jnp.int32, table.shape, 1)
    entries = jnp.where(place == 0, lcounts[FAR], jnp.where(place == 1, rcounts[FAR], 0))
    table[...] = jnp.where(place == 2, n_close, jnp.where(place == 3, n_close + n_far, entries))

    order = band_order(lax.axis_size("wide"))
    band = psi_band.shape[0]
    starts = [pl.multiple_of((here ^ shift) * band, band) for shift in order]

    total[...] = jnp.zeros_like(total)
    ph[NEAR], pl_[NEAR] = split(keep(near[...], lcounts[NEAR], rcounts[NEAR]))
    whole.wait()
    masked = keep(sbuf[...], lcounts[OWN], rcounts[OWN])
    ph[OWN], pl_[OWN] = split(masked)
    norm[...] = jnp.full(norm.shape, jnp.sum(masked * masked), F32)
    sbuf[...] = masked
    psi_band[...] = sbuf[pl.ds(pl.multiple_of(here * band, band), band), :]
    for p, start in enumerate(starts):
        psi[p * band : (p + 1) * band, :] = sbuf[pl.ds(start, band), :]

    for j in range(chans):
        kind = sum(jnp.where(places[c] == j, kinds[c], 0) for c in range(chans))
        lcount, rcount = pick(lcounts, kind), pick(rcounts, kind)
        for copy in copies[j]:
            copy.wait()

        def halve():
            rh[j], rl[j] = split(keep(rbuf[j], rcounts[OWN], rcount))
            for p, start in enumerate(starts):
                rows = slice(p * band, (p + 1) * band)
                piece = keep(lbuf[j, pl.ds(start, band), :], lcounts[OWN], lcount, start)
                lh[j, rows, :], ll[j, rows, :] = split(piece)

        @pl.when(kind <= NEAR)
        def _():
            halve()
            y = split(product((ph[kind], pl_[kind]), (rh[j], rl[j]), NT))
            total[...] += product((lh[j], ll[j]), y, NN)

        @pl.when(kind > NEAR)
        def _():
            halve()


def over_far(table, chans, group):
    first, have = table[0, 2], table[0, 3] - table[0, 2]
    for count in range(1, chans + 1):

        @pl.when(have == count)
        def _():
            group([first + i for i in range(count)])


def far_kernel(table, far, lh, ll, rh, rl, before, total, ph, pl_):
    rows = far.shape[0]

    @pl.when(table[0, 3] > table[0, 2])
    def _():
        ph[...], pl_[...] = split(keep(far[...], table[0, 0], table[0, 1]))

        def group(slots):
            psi = (ph[...], pl_[...])
            ys = [split(product(psi, (rh[j], rl[j]), NT)) for j in slots]
            terms = [product((lh[j, :, :rows], ll[j, :, :rows]), y, NN) for j, y in zip(slots, ys)]
            total[...] += functools.reduce(jnp.add, terms)

        over_far(table, lh.shape[0], group)


def last_kernel(table, far, lh, ll, rh, rl, before, psi, norm, *rest):
    *outs, total, ph, pl_ = rest
    rows = far.shape[0]
    block = psi.shape[0]
    total[...] = before[...]

    @pl.when(table[0, 3] > table[0, 2])
    def _():
        ph[...], pl_[...] = split(keep(far[...], table[0, 0], table[0, 1], block - rows))

        def group(slots):
            psi_far = (ph[...], pl_[...])
            ys = [split(product(psi_far, (rh[j], rl[j]), NT)) for j in slots]
            terms = [
                product((lh[j, :, block - rows :], ll[j, :, block - rows :]), y, NN) for j, y in zip(slots, ys)
            ]
            total[...] += functools.reduce(jnp.add, terms)

        over_far(table, lh.shape[0], group)

    row = lax.broadcasted_iota(jnp.int32, (TAIL, block), 0)
    sums = jnp.where(row == 0, jnp.sum(psi[...] * total[...]), norm[0, 0])
    size = outs[0].shape[0] - TAIL
    for i, out in enumerate(outs):
        out[:size, :] = total[i * size : (i + 1) * size, :]
        out[size:, :] = sums


def add_kernel(*refs):
    *parts, out = refs
    whole = parts[0][...]
    for part in parts[1:]:
        whole += part[...]
    out[...] = whole


def add_first_kernel(*refs):
    *parts, out = refs
    whole = parts[0][...]
    for part in parts[1:]:
        whole += part[...]
    row = lax.broadcasted_iota(jnp.int32, out.shape, 0)
    out[...] = jnp.where(row == 0, whole, parts[0][...])


def merge_kernel(*refs):
    *parts, sums, mine, give = refs
    half = mine.shape[0]
    whole = parts[0][: 2 * half, :]
    tail = parts[0][2 * half :, :128]
    first = tail
    for part in parts[1:]:
        whole += part[: 2 * half, :]
        first += part[2 * half :, :128]
    mine[...] = whole[:half]
    give[...] = whole[half:]
    row = lax.broadcasted_iota(jnp.int32, sums.shape, 0)
    sums[...] = jnp.where(row == 0, first, tail)


def halves_kernel(*refs):
    *parts, mine, give = refs
    half = mine.shape[0]
    whole = parts[0][...]
    for part in parts[1:]:
        whole += part[...]
    mine[...] = whole[:half]
    give[...] = whole[half:]


def final_kernel(n_parts, psi, *rest):
    parts, (*sums, out, alpha) = rest[:n_parts], rest[n_parts:]
    both = sums[0][0:2, :]
    for more in sums[1:]:
        both += more[0:2, :]
    ratio = both[0:1, :] / both[1:2, :]
    share = parts[0][...]
    for part in parts[1:]:
        share += part[...]
    out[...] = share - jnp.concatenate([ratio] * (psi.shape[1] // ratio.shape[1]), axis=1) * psi[...]
    alpha[...] = ratio


def exchange(value, axis, shift):
    count = lax.axis_size(axis)
    return lax.ppermute(value, axis, [(i, i ^ shift) for i in range(count)])


def f32(*shape):
    return jax.ShapeDtypeStruct(shape, F32)


def cost(flops, size=2**20):
    return pl.CostEstimate(flops=flops, bytes_accessed=size, transcendentals=0)


def call(kernel, out_shape, n_in, scratch=(), name=None, **more):
    return pl.pallas_call(
        kernel,
        out_shape=out_shape,
        in_specs=[VMEM] * n_in,
        out_specs=jax.tree.map(lambda _: VMEM, out_shape),
        scratch_shapes=scratch,
        compiler_params=pltpu.CompilerParams(vmem_limit_bytes=16 * 2**20),
        name=name,
        **more,
    )


def per_device(state, left_env, right_env, left_sizes, right_sizes, channel_charge):
    chans, _, block, _ = left_env.shape
    n_wide, n_narrow = lax.axis_size("wide"), lax.axis_size("narrow")
    band, half = block // n_wide, block // 2
    own = state[0]
    square, small = f32(block, block), f32(8, 128)
    work = 6 * chans * block**3

    ends = [(0, 0), (n_narrow - 1, n_narrow - 1)]
    across = [pair for k in range(1, n_narrow - 1, 2) for pair in ((k, k + 1), (k + 1, k))]
    far_top, far_low = (lax.ppermute(rows, "narrow", across + ends) for rows in (own[:half], own[half:]))
    near = exchange(own, "narrow", 1)

    halves = jax.ShapeDtypeStruct((chans, block, block), BF16)
    table, psi, psi_band, norm, lh, ll, rh, rl, total = pl.pallas_call(
        main_kernel,
        out_shape=[jax.ShapeDtypeStruct((8, 128), jnp.int32), square, f32(band, block), small]
        + [halves] * 4
        + [square],
        in_specs=[HBM] * 6 + [VMEM],
        out_specs=[VMEM] * 9,
        scratch_shapes=[
            pltpu.SMEM(left_sizes.shape, jnp.int32),
            pltpu.SMEM(right_sizes.shape, jnp.int32),
            pltpu.SMEM(channel_charge.shape, jnp.int32),
            pltpu.VMEM((chans, block, block), F32),
            pltpu.VMEM((chans, block, block), F32),
            pltpu.VMEM((block, block), F32),
            pltpu.VMEM((2, block, block), BF16),
            pltpu.VMEM((2, block, block), BF16),
            pltpu.SemaphoreType.DMA((2, chans)),
            pltpu.SemaphoreType.DMA((4,)),
        ],
        compiler_params=pltpu.CompilerParams(vmem_limit_bytes=32 * 2**20),
        cost_estimate=cost(work, 8 * chans * block * block),
        name="main",
    )(
        left_sizes, right_sizes, channel_charge,
        *(pltpu.with_memory_space_constraint(x, pltpu.HBM) for x in (state, left_env, right_env)),
        near,
    )
    envs = (lh, ll, rh, rl)

    pair = [pltpu.VMEM((half, block), BF16)] * 2
    total = call(far_kernel, square, 7, pair, name="far", cost_estimate=cost(work), input_output_aliases={6: 0})(table, far_top, *envs, total)

    groups = min(4, n_wide)
    held = n_wide // groups
    blocks = call(
        last_kernel, [f32(held * band + TAIL, block)] * groups, 9, [pltpu.VMEM((block, block), F32)] + pair,
        name="last", cost_estimate=cost(work),
    )(table, far_low, *envs, total, psi, norm)
    parts = [blocks[0]] + [exchange(blocks[s], "wide", s) for s in range(groups - 1, 0, -1)]

    held //= 2
    sums, mine, give = call(merge_kernel, [small] + [f32(held * band, block)] * 2, groups, name="merge")(*parts)
    step = groups
    while step < n_wide:
        sums = call(add_first_kernel, small, 2, name="wide", cost_estimate=cost(16 * block**3))(sums, exchange(sums, "wide", step))
        step *= 2
    parts = [mine, exchange(give, "wide", groups * held)]
    while held > 1:
        held //= 2
        mine, give = call(halves_kernel, [f32(held * band, block)] * 2, 2, name="halves")(*parts)
        parts = [mine, exchange(give, "wide", groups * held)]
    others = []
    if n_narrow <= 4:
        others = [exchange(sums, "narrow", s) for s in range(n_narrow - 1, 0, -1)]
    else:
        step = 1
        while step < n_narrow:
            sums = call(add_kernel, small, 2, name="sectors")(sums, exchange(sums, "narrow", step))
            step *= 2

    out, alpha = call(
        functools.partial(final_kernel, len(parts)), [f32(band, block), f32(1, 128)], 2 + len(parts) + len(others),
        name="final",
    )(psi_band, *parts, sums, *others)
    return out[None], alpha[0, 0]


def solution(mesh):
    placed = (
        P("narrow", None, None),
        P("wide", "narrow", None, None),
        P("wide", "narrow", None, None),
        P(),
        P(),
        P("wide"),
    )
    return jax.shard_map(
        per_device,
        mesh=mesh,
        in_specs=placed,
        out_specs=(P("narrow", "wide", None), P()),
        check_vma=False,
    )
```

```python
import functools

import jax
import jax.numpy as jnp
from jax import lax
from jax.experimental import pallas as pl
from jax.experimental.pallas import tpu as pltpu
from jax.sharding import PartitionSpec as P

F32 = jnp.float32
BF16 = jnp.bfloat16
NN = (((1,), (0,)), ((), ()))
NT = (((1,), (1,)), ((), ()))
VMEM = pl.BlockSpec(memory_space=pltpu.VMEM)
HBM = pl.BlockSpec(memory_space=pltpu.HBM)
OWN, NEAR, FAR, NONE = range(4)
TAIL = 8


def split(value):
    high = value.astype(BF16)
    low = (value - high.astype(F32)).astype(BF16)
    return high, low


def product(left, right, dims):
    (lh, ll), (rh, rl) = left, right
    dot = functools.partial(lax.dot_general, dimension_numbers=dims, preferred_element_type=F32)
    return dot(lh, rh) + (dot(lh, rl) + dot(ll, rh))


def keep(value, rows, cols, first_row=0):
    row = lax.broadcasted_iota(jnp.int32, value.shape, 0) + first_row
    col = lax.broadcasted_iota(jnp.int32, value.shape, 1)
    return jnp.where((row < rows) & (col < cols), value, 0.0)


def band_order(n_wide):
    groups = min(4, n_wide)
    return [s + groups * t for s in range(groups) for t in range(n_wide // groups)]


def main_kernel(
    lsz, rsz, charge, state, left, right, near,
    table, psi, psi_band, norm, lh, ll, rh, rl, total,
    ls, rs, cs, lbuf, rbuf, sbuf, ph, pl_, sems, more,
):
    chans, block = left.shape[0], state.shape[1]
    me, here = lax.axis_index("narrow"), lax.axis_index("wide")
    count = ls.shape[0]
    small = [
        pltpu.make_async_copy(src, dst, more.at[i])
        for i, (src, dst) in enumerate(((lsz, ls), (rsz, rs), (charge, cs)))
    ]
    whole = pltpu.make_async_copy(state.at[0], sbuf, more.at[3])
    for copy in small + [whole]:
        copy.start()
    for copy in small:
        copy.wait()

    side = 1 - 2 * lax.rem(me, 2)
    sectors = (me, me + side, me - side)

    def size_at(sizes, sector):
        inside = (sector >= 0) & (sector < count)
        return jnp.where(inside, sizes[jnp.clip(sector, 0, count - 1)], 0)

    lcounts = [size_at(ls, sector) for sector in sectors] + [0]
    rcounts = [size_at(rs, sector) for sector in sectors] + [0]

    def pick(values, kind):
        found = values[NONE]
        for i in (OWN, NEAR, FAR):
            found = jnp.where(kind == i, values[i], found)
        return found

    kinds = []
    for c in range(chans):
        src = me - (cs[c] - 1)
        kind = jnp.where(src == me, OWN, jnp.where(src == sectors[NEAR], NEAR, FAR))
        kinds.append(jnp.where((src >= 0) & (src < count), kind, NONE))
    places = [
        sum((kinds[o] < kinds[c]).astype(jnp.int32) for o in range(chans))
        + sum((kinds[o] == kinds[c]).astype(jnp.int32) for o in range(c))
        for c in range(chans)
    ]
    copies = []
    for j in range(chans):
        chan = sum(jnp.where(places[c] == j, c, 0) for c in range(chans))
        copies.append(
            (
                pltpu.make_async_copy(right.at[chan, 0], rbuf.at[j], sems.at[0, j]),
                pltpu.make_async_copy(left.at[chan, 0], lbuf.at[j], sems.at[1, j]),
            )
        )
        for copy in copies[-1]:
            copy.start()

    n_close = sum((k <= NEAR).astype(jnp.int32) for k in kinds)
    n_far = sum((k == FAR).astype(jnp.int32) for k in kinds)
    place = lax.broadcasted_iota(jnp.int32, table.shape, 1)
    entries = jnp.where(place == 0, lcounts[FAR], jnp.where(place == 1, rcounts[FAR], 0))
    table[...] = jnp.where(place == 2, n_close, jnp.where(place == 3, n_close + n_far, entries))

    order = band_order(lax.axis_size("wide"))
    band = psi_band.shape[0]
    starts = [pl.multiple_of((here ^ shift) * band, band) for shift in order]

    total[...] = jnp.zeros_like(total)
    ph[NEAR], pl_[NEAR] = split(keep(near[...], lcounts[NEAR], rcounts[NEAR]))
    whole.wait()
    masked = keep(sbuf[...], lcounts[OWN], rcounts[OWN])
    ph[OWN], pl_[OWN] = split(masked)
    norm[...] = jnp.full(norm.shape, jnp.sum(masked * masked), F32)
    sbuf[...] = masked
    psi_band[...] = sbuf[pl.ds(pl.multiple_of(here * band, band), band), :]
    for p, start in enumerate(starts):
        psi[p * band : (p + 1) * band, :] = sbuf[pl.ds(start, band), :]

    for j in range(chans):
        kind = sum(jnp.where(places[c] == j, kinds[c], 0) for c in range(chans))
        lcount, rcount = pick(lcounts, kind), pick(rcounts, kind)
        for copy in copies[j]:
            copy.wait()

        def halve():
            rh[j], rl[j] = split(keep(rbuf[j], rcounts[OWN], rcount))
            for p, start in enumerate(starts):
                rows = slice(p * band, (p + 1) * band)
                piece = keep(lbuf[j, pl.ds(start, band), :], lcounts[OWN], lcount, start)
                lh[j, rows, :], ll[j, rows, :] = split(piece)

        @pl.when(kind <= NEAR)
        def _():
            halve()
            y = split(product((ph[kind], pl_[kind]), (rh[j], rl[j]), NT))
            total[...] += product((lh[j], ll[j]), y, NN)

        @pl.when(kind > NEAR)
        def _():
            halve()


def over_far(table, chans, group):
    first, have = table[0, 2], table[0, 3] - table[0, 2]
    for count in range(1, chans + 1):

        @pl.when(have == count)
        def _():
            group([first + i for i in range(count)])


def far_kernel(table, far, lh, ll, rh, rl, before, total, ph, pl_):
    rows = far.shape[0]

    @pl.when(table[0, 3] > table[0, 2])
    def _():
        ph[...], pl_[...] = split(keep(far[...], table[0, 0], table[0, 1]))

        def group(slots):
            psi = (ph[...], pl_[...])
            ys = [split(product(psi, (rh[j], rl[j]), NT)) for j in slots]
            terms = [product((lh[j, :, :rows], ll[j, :, :rows]), y, NN) for j, y in zip(slots, ys)]
            total[...] += functools.reduce(jnp.add, terms)

        over_far(table, lh.shape[0], group)


def last_kernel(table, far, lh, ll, rh, rl, before, psi, norm, *rest):
    *outs, total, ph, pl_ = rest
    rows = far.shape[0]
    block = psi.shape[0]
    total[...] = before[...]

    @pl.when(table[0, 3] > table[0, 2])
    def _():
        ph[...], pl_[...] = split(keep(far[...], table[0, 0], table[0, 1], block - rows))

        def group(slots):
            psi_far = (ph[...], pl_[...])
            ys = [split(product(psi_far, (rh[j], rl[j]), NT)) for j in slots]
            terms = [
                product((lh[j, :, block - rows :], ll[j, :, block - rows :]), y, NN) for j, y in zip(slots, ys)
            ]
            total[...] += functools.reduce(jnp.add, terms)

        over_far(table, lh.shape[0], group)

    row = lax.broadcasted_iota(jnp.int32, (TAIL, block), 0)
    sums = jnp.where(row == 0, jnp.sum(psi[...] * total[...]), norm[0, 0])
    size = outs[0].shape[0] - TAIL
    for i, out in enumerate(outs):
        out[:size, :] = total[i * size : (i + 1) * size, :]
        out[size:, :] = sums


def add_kernel(*refs):
    *parts, out = refs
    whole = parts[0][...]
    for part in parts[1:]:
        whole += part[...]
    out[...] = whole


def add_first_kernel(*refs):
    *parts, out = refs
    whole = parts[0][...]
    for part in parts[1:]:
        whole += part[...]
    row = lax.broadcasted_iota(jnp.int32, out.shape, 0)
    out[...] = jnp.where(row == 0, whole, parts[0][...])


def merge_kernel(*refs):
    *parts, sums, mine, give = refs
    half = mine.shape[0]
    whole = parts[0][: 2 * half, :]
    tail = parts[0][2 * half :, :128]
    first = tail
    for part in parts[1:]:
        whole += part[: 2 * half, :]
        first += part[2 * half :, :128]
    mine[...] = whole[:half]
    give[...] = whole[half:]
    row = lax.broadcasted_iota(jnp.int32, sums.shape, 0)
    sums[...] = jnp.where(row == 0, first, tail)


def halves_kernel(*refs):
    *parts, mine, give = refs
    half = mine.shape[0]
    whole = parts[0][...]
    for part in parts[1:]:
        whole += part[...]
    mine[...] = whole[:half]
    give[...] = whole[half:]


def final_kernel(n_parts, psi, *rest):
    parts, (*sums, out, alpha) = rest[:n_parts], rest[n_parts:]
    both = sums[0][0:2, :]
    for more in sums[1:]:
        both += more[0:2, :]
    ratio = both[0:1, :] / both[1:2, :]
    share = parts[0][...]
    for part in parts[1:]:
        share += part[...]
    out[...] = share - jnp.concatenate([ratio] * (psi.shape[1] // ratio.shape[1]), axis=1) * psi[...]
    alpha[...] = ratio


def exchange(value, axis, shift):
    count = lax.axis_size(axis)
    return lax.ppermute(value, axis, [(i, i ^ shift) for i in range(count)])


def f32(*shape):
    return jax.ShapeDtypeStruct(shape, F32)


def cost(flops, size=2**20):
    return pl.CostEstimate(flops=flops, bytes_accessed=size, transcendentals=0)


def call(kernel, out_shape, n_in, scratch=(), name=None, **more):
    return pl.pallas_call(
        kernel,
        out_shape=out_shape,
        in_specs=[VMEM] * n_in,
        out_specs=jax.tree.map(lambda _: VMEM, out_shape),
        scratch_shapes=scratch,
        compiler_params=pltpu.CompilerParams(vmem_limit_bytes=16 * 2**20),
        name=name,
        **more,
    )


def per_device(state, left_env, right_env, left_sizes, right_sizes, channel_charge):
    chans, _, block, _ = left_env.shape
    n_wide, n_narrow = lax.axis_size("wide"), lax.axis_size("narrow")
    band, half = block // n_wide, block // 2
    own = state[0]
    square, small = f32(block, block), f32(8, 128)
    work = 6 * chans * block**3

    ends = [(0, 0), (n_narrow - 1, n_narrow - 1)]
    across = [pair for k in range(1, n_narrow - 1, 2) for pair in ((k, k + 1), (k + 1, k))]
    far_top, far_low = (lax.ppermute(rows, "narrow", across + ends) for rows in (own[:half], own[half:]))
    near = exchange(own, "narrow", 1)

    halves = jax.ShapeDtypeStruct((chans, block, block), BF16)
    table, psi, psi_band, norm, lh, ll, rh, rl, total = pl.pallas_call(
        main_kernel,
        out_shape=[jax.ShapeDtypeStruct((8, 128), jnp.int32), square, f32(band, block), small]
        + [halves] * 4
        + [square],
        in_specs=[HBM] * 6 + [VMEM],
        out_specs=[VMEM] * 9,
        scratch_shapes=[
            pltpu.SMEM(left_sizes.shape, jnp.int32),
            pltpu.SMEM(right_sizes.shape, jnp.int32),
            pltpu.SMEM(channel_charge.shape, jnp.int32),
            pltpu.VMEM((chans, block, block), F32),
            pltpu.VMEM((chans, block, block), F32),
            pltpu.VMEM((block, block), F32),
            pltpu.VMEM((2, block, block), BF16),
            pltpu.VMEM((2, block, block), BF16),
            pltpu.SemaphoreType.DMA((2, chans)),
            pltpu.SemaphoreType.DMA((4,)),
        ],
        compiler_params=pltpu.CompilerParams(vmem_limit_bytes=32 * 2**20),
        cost_estimate=cost(work, 8 * chans * block * block),
        name="main",
    )(
        left_sizes, right_sizes, channel_charge,
        *(pltpu.with_memory_space_constraint(x, pltpu.HBM) for x in (state, left_env, right_env)),
        near,
    )
    envs = (lh, ll, rh, rl)

    pair = [pltpu.VMEM((half, block), BF16)] * 2
    total = call(far_kernel, square, 7, pair, name="far", cost_estimate=cost(work), input_output_aliases={6: 0})(table, far_top, *envs, total)

    groups = min(4, n_wide)
    held = n_wide // groups
    blocks = call(
        last_kernel, [f32(held * band + TAIL, block)] * groups, 9, [pltpu.VMEM((block, block), F32)] + pair,
        name="last", cost_estimate=cost(work),
    )(table, far_low, *envs, total, psi, norm)
    parts = [blocks[0]] + [exchange(blocks[s], "wide", s) for s in range(groups - 1, 0, -1)]

    held //= 2
    sums, mine, give = call(merge_kernel, [small] + [f32(held * band, block)] * 2, groups, name="merge")(*parts)
    step = groups
    while step < n_wide:
        sums = call(add_first_kernel, small, 2, name="wide", cost_estimate=cost(16 * block**3))(sums, exchange(sums, "wide", step))
        step *= 2
    parts = [mine, exchange(give, "wide", groups * held)]
    while held > 1:
        held //= 2
        mine, give = call(halves_kernel, [f32(held * band, block)] * 2, 2, name="halves")(*parts)
        parts = [mine, exchange(give, "wide", groups * held)]
    others = []
    if n_narrow <= 4:
        others = [exchange(sums, "narrow", s) for s in (1, 2, 3)]
    else:
        step = 1
        while step < n_narrow:
            sums = call(add_kernel, small, 2, name="sectors")(sums, exchange(sums, "narrow", step))
            step *= 2

    out, alpha = call(
        functools.partial(final_kernel, len(parts)), [f32(band, block), f32(1, 128)], 2 + len(parts) + len(others),
        name="final",
    )(psi_band, *parts, sums, *others)
    return out[None], alpha[0, 0]


def solution(mesh):
    placed = (
        P("narrow", None, None),
        P("wide", "narrow", None, None),
        P("wide", "narrow", None, None),
        P(),
        P(),
        P("wide"),
    )
    return jax.shard_map(
        per_device,
        mesh=mesh,
        in_specs=placed,
        out_specs=(P("narrow", "wide", None), P()),
        check_vma=False,
    )
```

```python
import functools

import jax
import jax.numpy as jnp
from jax import lax
from jax.experimental import pallas as pl
from jax.experimental.pallas import tpu as pltpu
from jax.sharding import PartitionSpec as P

F32 = jnp.float32
BF16 = jnp.bfloat16
NN = (((1,), (0,)), ((), ()))
NT = (((1,), (1,)), ((), ()))
VMEM = pl.BlockSpec(memory_space=pltpu.VMEM)
HBM = pl.BlockSpec(memory_space=pltpu.HBM)
OWN, NEAR, FAR, NONE = range(4)
TAIL = 8


def split(value):
    high = value.astype(BF16)
    low = (value - high.astype(F32)).astype(BF16)
    return high, low


def product(left, right, dims):
    (lh, ll), (rh, rl) = left, right
    dot = functools.partial(lax.dot_general, dimension_numbers=dims, preferred_element_type=F32)
    return dot(lh, rh) + (dot(lh, rl) + dot(ll, rh))


def keep(value, rows, cols, first_row=0):
    row = lax.broadcasted_iota(jnp.int32, value.shape, 0) + first_row
    col = lax.broadcasted_iota(jnp.int32, value.shape, 1)
    return jnp.where((row < rows) & (col < cols), value, 0.0)


def band_order(n_wide):
    groups = min(4, n_wide)
    return [s + groups * t for s in range(groups) for t in range(n_wide // groups)]


def main_kernel(
    lsz, rsz, charge, state, left, right, near,
    table, psi, psi_band, norm, lh, ll, rh, rl, total,
    ls, rs, cs, lbuf, rbuf, sbuf, ph, pl_, sems, more,
):
    chans, block = left.shape[0], state.shape[1]
    me, here = lax.axis_index("narrow"), lax.axis_index("wide")
    count = ls.shape[0]
    small = [
        pltpu.make_async_copy(src, dst, more.at[i])
        for i, (src, dst) in enumerate(((lsz, ls), (rsz, rs), (charge, cs)))
    ]
    whole = pltpu.make_async_copy(state.at[0], sbuf, more.at[3])
    for copy in small + [whole]:
        copy.start()
    for copy in small:
        copy.wait()

    side = 1 - 2 * lax.rem(me, 2)
    sectors = (me, me + side, me - side)

    def size_at(sizes, sector):
        inside = (sector >= 0) & (sector < count)
        return jnp.where(inside, sizes[jnp.clip(sector, 0, count - 1)], 0)

    lcounts = [size_at(ls, sector) for sector in sectors] + [0]
    rcounts = [size_at(rs, sector) for sector in sectors] + [0]

    def pick(values, kind):
        found = values[NONE]
        for i in (OWN, NEAR, FAR):
            found = jnp.where(kind == i, values[i], found)
        return found

    kinds = []
    for c in range(chans):
        src = me - (cs[c] - 1)
        kind = jnp.where(src == me, OWN, jnp.where(src == sectors[NEAR], NEAR, FAR))
        kinds.append(jnp.where((src >= 0) & (src < count), kind, NONE))
    places = [
        sum((kinds[o] < kinds[c]).astype(jnp.int32) for o in range(chans))
        + sum((kinds[o] == kinds[c]).astype(jnp.int32) for o in range(c))
        for c in range(chans)
    ]
    copies = []
    for j in range(chans):
        chan = sum(jnp.where(places[c] == j, c, 0) for c in range(chans))
        copies.append(
            (
                pltpu.make_async_copy(right.at[chan, 0], rbuf.at[j], sems.at[0, j]),
                pltpu.make_async_copy(left.at[chan, 0], lbuf.at[j], sems.at[1, j]),
            )
        )
        for copy in copies[-1]:
            copy.start()

    n_close = sum((k <= NEAR).astype(jnp.int32) for k in kinds)
    n_far = sum((k == FAR).astype(jnp.int32) for k in kinds)
    place = lax.broadcasted_iota(jnp.int32, table.shape, 1)
    entries = jnp.where(place == 0, lcounts[FAR], jnp.where(place == 1, rcounts[FAR], 0))
    table[...] = jnp.where(place == 2, n_close, jnp.where(place == 3, n_close + n_far, entries))

    order = band_order(lax.axis_size("wide"))
    band = psi_band.shape[0]
    starts = [pl.multiple_of((here ^ shift) * band, band) for shift in order]

    total[...] = jnp.zeros_like(total)
    ph[NEAR], pl_[NEAR] = split(keep(near[...], lcounts[NEAR], rcounts[NEAR]))
    whole.wait()
    masked = keep(sbuf[...], lcounts[OWN], rcounts[OWN])
    ph[OWN], pl_[OWN] = split(masked)
    norm[...] = jnp.full(norm.shape, jnp.sum(masked * masked), F32)
    sbuf[...] = masked
    psi_band[...] = sbuf[pl.ds(pl.multiple_of(here * band, band), band), :]
    for p, start in enumerate(starts):
        psi[p * band : (p + 1) * band, :] = sbuf[pl.ds(start, band), :]

    for j in range(chans):
        kind = sum(jnp.where(places[c] == j, kinds[c], 0) for c in range(chans))
        lcount, rcount = pick(lcounts, kind), pick(rcounts, kind)
        for copy in copies[j]:
            copy.wait()

        def halve():
            rh[j], rl[j] = split(keep(rbuf[j], rcounts[OWN], rcount))
            for p, start in enumerate(starts):
                rows = slice(p * band, (p + 1) * band)
                piece = keep(lbuf[j, pl.ds(start, band), :], lcounts[OWN], lcount, start)
                lh[j, rows, :], ll[j, rows, :] = split(piece)

        @pl.when(kind <= NEAR)
        def _():
            halve()
            y = split(product((ph[kind], pl_[kind]), (rh[j], rl[j]), NT))
            total[...] += product((lh[j], ll[j]), y, NN)

        @pl.when(kind > NEAR)
        def _():
            halve()


def over_far(table, chans, group):
    first, have = table[0, 2], table[0, 3] - table[0, 2]
    for count in range(1, chans + 1):

        @pl.when(have == count)
        def _():
            group([first + i for i in range(count)])


def far_kernel(table, far, lh, ll, rh, rl, before, total, ph, pl_):
    rows = far.shape[0]

    @pl.when(table[0, 3] > table[0, 2])
    def _():
        ph[...], pl_[...] = split(keep(far[...], table[0, 0], table[0, 1]))

        def group(slots):
            psi = (ph[...], pl_[...])
            ys = [split(product(psi, (rh[j], rl[j]), NT)) for j in slots]
            terms = [product((lh[j, :, :rows], ll[j, :, :rows]), y, NN) for j, y in zip(slots, ys)]
            total[...] += functools.reduce(jnp.add, terms)

        over_far(table, lh.shape[0], group)


def last_kernel(table, far, lh, ll, rh, rl, before, psi, norm, *rest):
    *outs, total, ph, pl_ = rest
    rows = far.shape[0]
    block = psi.shape[0]

    @pl.when(table[0, 3] == table[0, 2])
    def _():
        total[...] = before[...]

    @pl.when(table[0, 3] > table[0, 2])
    def _():
        ph[...], pl_[...] = split(keep(far[...], table[0, 0], table[0, 1], block - rows))

        def group(slots):
            psi_far = (ph[...], pl_[...])
            ys = [split(product(psi_far, (rh[j], rl[j]), NT)) for j in slots]
            terms = [
                product((lh[j, :, block - rows :], ll[j, :, block - rows :]), y, NN) for j, y in zip(slots, ys)
            ]
            total[...] = before[...] + functools.reduce(jnp.add, terms)

        over_far(table, lh.shape[0], group)

    row = lax.broadcasted_iota(jnp.int32, (TAIL, block), 0)
    sums = jnp.where(row == 0, jnp.sum(psi[...] * total[...]), norm[0, 0])
    size = outs[0].shape[0] - TAIL
    for i, out in enumerate(outs):
        out[:size, :] = total[i * size : (i + 1) * size, :]
        out[size:, :] = sums


def add_kernel(*refs):
    *parts, out = refs
    whole = parts[0][...]
    for part in parts[1:]:
        whole += part[...]
    out[...] = whole


def add_first_kernel(*refs):
    *parts, out = refs
    whole = parts[0][...]
    for part in parts[1:]:
        whole += part[...]
    row = lax.broadcasted_iota(jnp.int32, out.shape, 0)
    out[...] = jnp.where(row == 0, whole, parts[0][...])


def merge_kernel(*refs):
    *parts, sums, mine, give = refs
    half = mine.shape[0]
    whole = parts[0][: 2 * half, :]
    tail = parts[0][2 * half :, :128]
    first = tail
    for part in parts[1:]:
        whole += part[: 2 * half, :]
        first += part[2 * half :, :128]
    mine[...] = whole[:half]
    give[...] = whole[half:]
    row = lax.broadcasted_iota(jnp.int32, sums.shape, 0)
    sums[...] = jnp.where(row == 0, first, tail)


def halves_kernel(*refs):
    *parts, mine, give = refs
    half = mine.shape[0]
    whole = parts[0][...]
    for part in parts[1:]:
        whole += part[...]
    mine[...] = whole[:half]
    give[...] = whole[half:]


def final_kernel(n_parts, psi, *rest):
    parts, (*sums, out, alpha) = rest[:n_parts], rest[n_parts:]
    both = sums[0][0:2, :]
    for more in sums[1:]:
        both += more[0:2, :]
    ratio = both[0:1, :] / both[1:2, :]
    share = parts[0][...]
    for part in parts[1:]:
        share += part[...]
    out[...] = share - jnp.concatenate([ratio] * (psi.shape[1] // ratio.shape[1]), axis=1) * psi[...]
    alpha[...] = ratio


def exchange(value, axis, shift):
    count = lax.axis_size(axis)
    return lax.ppermute(value, axis, [(i, i ^ shift) for i in range(count)])


def f32(*shape):
    return jax.ShapeDtypeStruct(shape, F32)


def cost(flops, size=2**20):
    return pl.CostEstimate(flops=flops, bytes_accessed=size, transcendentals=0)


def call(kernel, out_shape, n_in, scratch=(), name=None, **more):
    return pl.pallas_call(
        kernel,
        out_shape=out_shape,
        in_specs=[VMEM] * n_in,
        out_specs=jax.tree.map(lambda _: VMEM, out_shape),
        scratch_shapes=scratch,
        compiler_params=pltpu.CompilerParams(vmem_limit_bytes=16 * 2**20),
        name=name,
        **more,
    )


def per_device(state, left_env, right_env, left_sizes, right_sizes, channel_charge):
    chans, _, block, _ = left_env.shape
    n_wide, n_narrow = lax.axis_size("wide"), lax.axis_size("narrow")
    band, half = block // n_wide, block // 2
    own = state[0]
    square, small = f32(block, block), f32(8, 128)
    work = 6 * chans * block**3

    ends = [(0, 0), (n_narrow - 1, n_narrow - 1)]
    across = [pair for k in range(1, n_narrow - 1, 2) for pair in ((k, k + 1), (k + 1, k))]
    far_top, far_low = (lax.ppermute(rows, "narrow", across + ends) for rows in (own[:half], own[half:]))
    near = exchange(own, "narrow", 1)

    halves = jax.ShapeDtypeStruct((chans, block, block), BF16)
    table, psi, psi_band, norm, lh, ll, rh, rl, total = pl.pallas_call(
        main_kernel,
        out_shape=[jax.ShapeDtypeStruct((8, 128), jnp.int32), square, f32(band, block), small]
        + [halves] * 4
        + [square],
        in_specs=[HBM] * 6 + [VMEM],
        out_specs=[VMEM] * 9,
        scratch_shapes=[
            pltpu.SMEM(left_sizes.shape, jnp.int32),
            pltpu.SMEM(right_sizes.shape, jnp.int32),
            pltpu.SMEM(channel_charge.shape, jnp.int32),
            pltpu.VMEM((chans, block, block), F32),
            pltpu.VMEM((chans, block, block), F32),
            pltpu.VMEM((block, block), F32),
            pltpu.VMEM((2, block, block), BF16),
            pltpu.VMEM((2, block, block), BF16),
            pltpu.SemaphoreType.DMA((2, chans)),
            pltpu.SemaphoreType.DMA((4,)),
        ],
        compiler_params=pltpu.CompilerParams(vmem_limit_bytes=32 * 2**20),
        cost_estimate=cost(work, 8 * chans * block * block),
        name="main",
    )(
        left_sizes, right_sizes, channel_charge,
        *(pltpu.with_memory_space_constraint(x, pltpu.HBM) for x in (state, left_env, right_env)),
        near,
    )
    envs = (lh, ll, rh, rl)

    pair = [pltpu.VMEM((half, block), BF16)] * 2
    total = call(far_kernel, square, 7, pair, name="far", cost_estimate=cost(work), input_output_aliases={6: 0})(table, far_top, *envs, total)

    groups = min(4, n_wide)
    held = n_wide // groups
    blocks = call(
        last_kernel, [f32(held * band + TAIL, block)] * groups, 9, [pltpu.VMEM((block, block), F32)] + pair,
        name="last", cost_estimate=cost(work),
    )(table, far_low, *envs, total, psi, norm)
    parts = [blocks[0]] + [exchange(blocks[s], "wide", s) for s in range(groups - 1, 0, -1)]

    held //= 2
    sums, mine, give = call(merge_kernel, [small] + [f32(held * band, block)] * 2, groups, name="merge")(*parts)
    step = groups
    while step < n_wide:
        sums = call(add_first_kernel, small, 2, name="wide", cost_estimate=cost(16 * block**3))(sums, exchange(sums, "wide", step))
        step *= 2
    parts = [mine, exchange(give, "wide", groups * held)]
    while held > 1:
        held //= 2
        mine, give = call(halves_kernel, [f32(held * band, block)] * 2, 2, name="halves")(*parts)
        parts = [mine, exchange(give, "wide", groups * held)]
    others = []
    for step in ([3] if n_narrow >= 4 else []) + [1] + [1 << bit for bit in range(2, n_narrow.bit_length() - 1)]:
        if others:
            sums = call(add_kernel, small, 2, name="sectors")(sums, *others)
        others = [exchange(sums, "narrow", step)]

    out, alpha = call(
        functools.partial(final_kernel, len(parts)), [f32(band, block), f32(1, 128)], 2 + len(parts) + len(others),
        name="final",
    )(psi_band, *parts, sums, *others)
    return out[None], alpha[0, 0]


def solution(mesh):
    placed = (
        P("narrow", None, None),
        P("wide", "narrow", None, None),
        P("wide", "narrow", None, None),
        P(),
        P(),
        P("wide"),
    )
    return jax.shard_map(
        per_device,
        mesh=mesh,
        in_specs=placed,
        out_specs=(P("narrow", "wide", None), P()),
        check_vma=False,
    )
```

```python
import functools

import jax
import jax.numpy as jnp
from jax import lax
from jax.experimental import pallas as pl
from jax.experimental.pallas import tpu as pltpu
from jax.sharding import PartitionSpec as P

F32 = jnp.float32
BF16 = jnp.bfloat16
NN = (((1,), (0,)), ((), ()))
NT = (((1,), (1,)), ((), ()))
VMEM = pl.BlockSpec(memory_space=pltpu.VMEM)
HBM = pl.BlockSpec(memory_space=pltpu.HBM)
OWN, NEAR, FAR, NONE = range(4)
TAIL = 8


def split(value):
    high = value.astype(BF16)
    low = (value - high.astype(F32)).astype(BF16)
    return high, low


def product(left, right, dims):
    (lh, ll), (rh, rl) = left, right
    dot = functools.partial(lax.dot_general, dimension_numbers=dims, preferred_element_type=F32)
    return dot(lh, rh) + (dot(lh, rl) + dot(ll, rh))


def keep(value, rows, cols, first_row=0):
    row = lax.broadcasted_iota(jnp.int32, value.shape, 0) + first_row
    col = lax.broadcasted_iota(jnp.int32, value.shape, 1)
    return jnp.where((row < rows) & (col < cols), value, 0.0)


def band_order(n_wide):
    groups = min(4, n_wide)
    return [s + groups * t for s in range(groups) for t in range(n_wide // groups)]


def main_kernel(
    lsz, rsz, charge, state, left, right, near,
    table, psi, psi_band, norm, lh, ll, rh, rl, total,
    ls, rs, cs, lbuf, rbuf, sbuf, ph, pl_, sems, more,
):
    chans, block = left.shape[0], state.shape[1]
    me, here = lax.axis_index("narrow"), lax.axis_index("wide")
    count = ls.shape[0]
    small = [
        pltpu.make_async_copy(src, dst, more.at[i])
        for i, (src, dst) in enumerate(((lsz, ls), (rsz, rs), (charge, cs)))
    ]
    whole = pltpu.make_async_copy(state.at[0], sbuf, more.at[3])
    for copy in small + [whole]:
        copy.start()
    for copy in small:
        copy.wait()

    side = 1 - 2 * lax.rem(me, 2)
    sectors = (me, me + side, me - side)

    def size_at(sizes, sector):
        inside = (sector >= 0) & (sector < count)
        return jnp.where(inside, sizes[jnp.clip(sector, 0, count - 1)], 0)

    lcounts = [size_at(ls, sector) for sector in sectors] + [0]
    rcounts = [size_at(rs, sector) for sector in sectors] + [0]

    def pick(values, kind):
        found = values[NONE]
        for i in (OWN, NEAR, FAR):
            found = jnp.where(kind == i, values[i], found)
        return found

    kinds = []
    for c in range(chans):
        src = me - (cs[c] - 1)
        kind = jnp.where(src == me, OWN, jnp.where(src == sectors[NEAR], NEAR, FAR))
        kinds.append(jnp.where((src >= 0) & (src < count), kind, NONE))
    places = [
        sum((kinds[o] < kinds[c]).astype(jnp.int32) for o in range(chans))
        + sum((kinds[o] == kinds[c]).astype(jnp.int32) for o in range(c))
        for c in range(chans)
    ]
    copies = []
    for j in range(chans):
        chan = sum(jnp.where(places[c] == j, c, 0) for c in range(chans))
        copies.append(
            (
                pltpu.make_async_copy(right.at[chan, 0], rbuf.at[j], sems.at[0, j]),
                pltpu.make_async_copy(left.at[chan, 0], lbuf.at[j], sems.at[1, j]),
            )
        )
        for copy in copies[-1]:
            copy.start()

    n_close = sum((k <= NEAR).astype(jnp.int32) for k in kinds)
    n_far = sum((k == FAR).astype(jnp.int32) for k in kinds)
    place = lax.broadcasted_iota(jnp.int32, table.shape, 1)
    entries = jnp.where(place == 0, lcounts[FAR], jnp.where(place == 1, rcounts[FAR], 0))
    table[...] = jnp.where(place == 2, n_close, jnp.where(place == 3, n_close + n_far, entries))

    order = band_order(lax.axis_size("wide"))
    band = psi_band.shape[0]
    starts = [pl.multiple_of((here ^ shift) * band, band) for shift in order]

    total[...] = jnp.zeros_like(total)
    ph[NEAR], pl_[NEAR] = split(keep(near[...], lcounts[NEAR], rcounts[NEAR]))
    whole.wait()
    masked = keep(sbuf[...], lcounts[OWN], rcounts[OWN])
    ph[OWN], pl_[OWN] = split(masked)
    norm[...] = jnp.full(norm.shape, jnp.sum(masked * masked), F32)
    sbuf[...] = masked
    psi_band[...] = sbuf[pl.ds(pl.multiple_of(here * band, band), band), :]
    for p, start in enumerate(starts):
        psi[p * band : (p + 1) * band, :] = sbuf[pl.ds(start, band), :]

    for j in range(chans):
        kind = sum(jnp.where(places[c] == j, kinds[c], 0) for c in range(chans))
        lcount, rcount = pick(lcounts, kind), pick(rcounts, kind)
        for copy in copies[j]:
            copy.wait()

        def halve():
            rh[j], rl[j] = split(keep(rbuf[j], rcounts[OWN], rcount))
            for p, start in enumerate(starts):
                rows = slice(p * band, (p + 1) * band)
                piece = keep(lbuf[j, pl.ds(start, band), :], lcounts[OWN], lcount, start)
                lh[j, rows, :], ll[j, rows, :] = split(piece)

        @pl.when(kind <= NEAR)
        def _():
            halve()
            y = split(product((ph[kind], pl_[kind]), (rh[j], rl[j]), NT))
            total[...] += product((lh[j], ll[j]), y, NN)

        @pl.when(kind > NEAR)
        def _():
            halve()


def over_far(table, chans, group):
    first, have = table[0, 2], table[0, 3] - table[0, 2]
    for count in range(1, chans + 1):

        @pl.when(have == count)
        def _():
            group([first + i for i in range(count)])


def far_kernel(table, far, lh, ll, rh, rl, before, total, ph, pl_):
    rows = far.shape[0]

    @pl.when(table[0, 3] > table[0, 2])
    def _():
        ph[...], pl_[...] = split(keep(far[...], table[0, 0], table[0, 1]))

        def group(slots):
            psi = (ph[...], pl_[...])
            ys = [split(product(psi, (rh[j], rl[j]), NT)) for j in slots]
            terms = [product((lh[j, :, :rows], ll[j, :, :rows]), y, NN) for j, y in zip(slots, ys)]
            total[...] += functools.reduce(jnp.add, terms)

        over_far(table, lh.shape[0], group)


def last_kernel(table, far, lh, ll, rh, rl, before, psi, norm, *rest):
    *outs, total, ph, pl_ = rest
    rows = far.shape[0]
    block = psi.shape[0]

    @pl.when(table[0, 3] == table[0, 2])
    def _():
        total[...] = before[...]

    @pl.when(table[0, 3] > table[0, 2])
    def _():
        ph[...], pl_[...] = split(keep(far[...], table[0, 0], table[0, 1], block - rows))

        def group(slots):
            psi_far = (ph[...], pl_[...])
            ys = [split(product(psi_far, (rh[j], rl[j]), NT)) for j in slots]
            terms = [
                product((lh[j, :, block - rows :], ll[j, :, block - rows :]), y, NN) for j, y in zip(slots, ys)
            ]
            total[...] = before[...] + functools.reduce(jnp.add, terms)

        over_far(table, lh.shape[0], group)

    row = lax.broadcasted_iota(jnp.int32, (TAIL, block), 0)
    sums = jnp.where(row == 0, jnp.sum(psi[...] * total[...]), norm[0, 0])
    size = outs[0].shape[0] - TAIL
    for i, out in enumerate(outs):
        out[:size, :] = total[i * size : (i + 1) * size, :]
        out[size:, :] = sums


def add_kernel(*refs):
    *parts, out = refs
    whole = parts[0][...]
    for part in parts[1:]:
        whole += part[...]
    out[...] = whole


def add_first_kernel(*refs):
    *parts, out = refs
    whole = parts[0][...]
    for part in parts[1:]:
        whole += part[...]
    row = lax.broadcasted_iota(jnp.int32, out.shape, 0)
    out[...] = jnp.where(row == 0, whole, parts[0][...])


def merge_kernel(*refs):
    *parts, sums, mine, give = refs
    half = mine.shape[0]
    whole = parts[0][: 2 * half, :]
    tail = parts[0][2 * half :, :128]
    first = tail
    for part in parts[1:]:
        whole += part[: 2 * half, :]
        first += part[2 * half :, :128]
    mine[...] = whole[:half]
    give[...] = whole[half:]
    row = lax.broadcasted_iota(jnp.int32, sums.shape, 0)
    sums[...] = jnp.where(row == 0, first, tail)


def halves_kernel(*refs):
    *parts, mine, give = refs
    half = mine.shape[0]
    whole = parts[0][...]
    for part in parts[1:]:
        whole += part[...]
    mine[...] = whole[:half]
    give[...] = whole[half:]


def final_kernel(n_parts, psi, *rest):
    parts, (*sums, out, alpha) = rest[:n_parts], rest[n_parts:]
    both = sums[0][0:2, :]
    for more in sums[1:]:
        both += more[0:2, :]
    ratio = both[0:1, :] / both[1:2, :]
    share = parts[0][...]
    for part in parts[1:]:
        share += part[...]
    out[...] = share - jnp.concatenate([ratio] * (psi.shape[1] // ratio.shape[1]), axis=1) * psi[...]
    alpha[...] = ratio


def exchange(value, axis, shift):
    count = lax.axis_size(axis)
    return lax.ppermute(value, axis, [(i, i ^ shift) for i in range(count)])


def f32(*shape):
    return jax.ShapeDtypeStruct(shape, F32)


def cost(flops, size=2**20):
    return pl.CostEstimate(flops=flops, bytes_accessed=size, transcendentals=0)


def call(kernel, out_shape, n_in, scratch=(), name=None, **more):
    return pl.pallas_call(
        kernel,
        out_shape=out_shape,
        in_specs=[VMEM] * n_in,
        out_specs=jax.tree.map(lambda _: VMEM, out_shape),
        scratch_shapes=scratch,
        compiler_params=pltpu.CompilerParams(vmem_limit_bytes=16 * 2**20),
        name=name,
        **more,
    )


def per_device(state, left_env, right_env, left_sizes, right_sizes, channel_charge):
    chans, _, block, _ = left_env.shape
    n_wide, n_narrow = lax.axis_size("wide"), lax.axis_size("narrow")
    band, half = block // n_wide, block // 2
    own = state[0]
    square, small = f32(block, block), f32(8, 128)
    work = 6 * chans * block**3

    across = [pair for k in range(1, n_narrow - 1, 2) for pair in ((k, k + 1), (k + 1, k))]
    far_top, far_low = (lax.ppermute(rows, "narrow", across) for rows in (own[:half], own[half:]))
    near = exchange(own, "narrow", 1)

    halves = jax.ShapeDtypeStruct((chans, block, block), BF16)
    table, psi, psi_band, norm, lh, ll, rh, rl, total = pl.pallas_call(
        main_kernel,
        out_shape=[jax.ShapeDtypeStruct((8, 128), jnp.int32), square, f32(band, block), small]
        + [halves] * 4
        + [square],
        in_specs=[HBM] * 6 + [VMEM],
        out_specs=[VMEM] * 9,
        scratch_shapes=[
            pltpu.SMEM(left_sizes.shape, jnp.int32),
            pltpu.SMEM(right_sizes.shape, jnp.int32),
            pltpu.SMEM(channel_charge.shape, jnp.int32),
            pltpu.VMEM((chans, block, block), F32),
            pltpu.VMEM((chans, block, block), F32),
            pltpu.VMEM((block, block), F32),
            pltpu.VMEM((2, block, block), BF16),
            pltpu.VMEM((2, block, block), BF16),
            pltpu.SemaphoreType.DMA((2, chans)),
            pltpu.SemaphoreType.DMA((4,)),
        ],
        compiler_params=pltpu.CompilerParams(vmem_limit_bytes=32 * 2**20),
        cost_estimate=cost(work, 8 * chans * block * block),
        name="main",
    )(
        left_sizes, right_sizes, channel_charge,
        *(pltpu.with_memory_space_constraint(x, pltpu.HBM) for x in (state, left_env, right_env)),
        near,
    )
    envs = (lh, ll, rh, rl)

    pair = [pltpu.VMEM((half, block), BF16)] * 2
    total = call(far_kernel, square, 7, pair, name="far", cost_estimate=cost(work), input_output_aliases={6: 0})(table, far_top, *envs, total)

    groups = min(4, n_wide)
    held = n_wide // groups
    blocks = call(
        last_kernel, [f32(held * band + TAIL, block)] * groups, 9, [pltpu.VMEM((block, block), F32)] + pair,
        name="last", cost_estimate=cost(work),
    )(table, far_low, *envs, total, psi, norm)
    parts = [blocks[0]] + [exchange(blocks[s], "wide", s) for s in range(groups - 1, 0, -1)]

    held //= 2
    sums, mine, give = call(merge_kernel, [small] + [f32(held * band, block)] * 2, groups, name="merge")(*parts)
    step = groups
    while step < n_wide:
        sums = call(add_first_kernel, small, 2, name="wide", cost_estimate=cost(16 * block**3))(sums, exchange(sums, "wide", step))
        step *= 2
    parts = [mine, exchange(give, "wide", groups * held)]
    while held > 1:
        held //= 2
        mine, give = call(halves_kernel, [f32(held * band, block)] * 2, 2, name="halves")(*parts)
        parts = [mine, exchange(give, "wide", groups * held)]
    others = []
    for step in ([3] if n_narrow >= 4 else []) + [1] + [1 << bit for bit in range(2, n_narrow.bit_length() - 1)]:
        if others:
            sums = call(add_kernel, small, 2, name="sectors")(sums, *others)
        others = [exchange(sums, "narrow", step)]

    out, alpha = call(
        functools.partial(final_kernel, len(parts)), [f32(band, block), f32(1, 128)], 2 + len(parts) + len(others),
        name="final",
    )(psi_band, *parts, sums, *others)
    return out[None], alpha[0, 0]


def solution(mesh):
    placed = (
        P("narrow", None, None),
        P("wide", "narrow", None, None),
        P("wide", "narrow", None, None),
        P(),
        P(),
        P("wide"),
    )
    return jax.shard_map(
        per_device,
        mesh=mesh,
        in_specs=placed,
        out_specs=(P("narrow", "wide", None), P()),
        check_vma=False,
    )
```

```python
import functools

import jax
import jax.numpy as jnp
from jax import lax
from jax.experimental import pallas as pl
from jax.experimental.pallas import tpu as pltpu
from jax.sharding import PartitionSpec as P

F32 = jnp.float32
BF16 = jnp.bfloat16
NN = (((1,), (0,)), ((), ()))
NT = (((1,), (1,)), ((), ()))
VMEM = pl.BlockSpec(memory_space=pltpu.VMEM)
HBM = pl.BlockSpec(memory_space=pltpu.HBM)
OWN, NEAR, FAR, NONE = range(4)
TAIL = 8


def split(value):
    high = value.astype(BF16)
    low = (value - high.astype(F32)).astype(BF16)
    return high, low


def product(left, right, dims):
    (lh, ll), (rh, rl) = left, right
    dot = functools.partial(lax.dot_general, dimension_numbers=dims, preferred_element_type=F32)
    return dot(lh, rh) + (dot(lh, rl) + dot(ll, rh))


def keep(value, rows, cols, first_row=0):
    row = lax.broadcasted_iota(jnp.int32, value.shape, 0) + first_row
    col = lax.broadcasted_iota(jnp.int32, value.shape, 1)
    return jnp.where((row < rows) & (col < cols), value, 0.0)


def band_order(n_wide):
    groups = min(4, n_wide)
    return [s + groups * t for s in range(groups) for t in range(n_wide // groups)]


def main_kernel(
    lsz, rsz, charge, state, left, right, near,
    table, psi, psi_band, norm, lh, ll, rh, rl, total,
    ls, rs, cs, lbuf, rbuf, sbuf, ph, pl_, sems, more,
):
    chans, block = left.shape[0], state.shape[1]
    me, here = lax.axis_index("narrow"), lax.axis_index("wide")
    count = ls.shape[0]
    small = [
        pltpu.make_async_copy(src, dst, more.at[i])
        for i, (src, dst) in enumerate(((lsz, ls), (rsz, rs), (charge, cs)))
    ]
    whole = pltpu.make_async_copy(state.at[0], sbuf, more.at[3])
    for copy in small + [whole]:
        copy.start()
    for copy in small:
        copy.wait()

    side = 1 - 2 * lax.rem(me, 2)
    sectors = (me, me + side, me - side)

    def size_at(sizes, sector):
        inside = (sector >= 0) & (sector < count)
        return jnp.where(inside, sizes[jnp.clip(sector, 0, count - 1)], 0)

    lcounts = [size_at(ls, sector) for sector in sectors] + [0]
    rcounts = [size_at(rs, sector) for sector in sectors] + [0]

    def pick(values, kind):
        found = values[NONE]
        for i in (OWN, NEAR, FAR):
            found = jnp.where(kind == i, values[i], found)
        return found

    kinds = []
    for c in range(chans):
        src = me - (cs[c] - 1)
        kind = jnp.where(src == me, OWN, jnp.where(src == sectors[NEAR], NEAR, FAR))
        kinds.append(jnp.where((src >= 0) & (src < count), kind, NONE))
    places = [
        sum((kinds[o] < kinds[c]).astype(jnp.int32) for o in range(chans))
        + sum((kinds[o] == kinds[c]).astype(jnp.int32) for o in range(c))
        for c in range(chans)
    ]
    copies = []
    for j in range(chans):
        chan = sum(jnp.where(places[c] == j, c, 0) for c in range(chans))
        copies.append(
            (
                pltpu.make_async_copy(right.at[chan, 0], rbuf.at[j], sems.at[0, j]),
                pltpu.make_async_copy(left.at[chan, 0], lbuf.at[j], sems.at[1, j]),
            )
        )
        for copy in copies[-1]:
            copy.start()

    n_close = sum((k <= NEAR).astype(jnp.int32) for k in kinds)
    n_far = sum((k == FAR).astype(jnp.int32) for k in kinds)
    place = lax.broadcasted_iota(jnp.int32, table.shape, 1)
    entries = jnp.where(place == 0, lcounts[FAR], jnp.where(place == 1, rcounts[FAR], 0))
    table[...] = jnp.where(place == 2, n_close, jnp.where(place == 3, n_close + n_far, entries))

    order = band_order(lax.axis_size("wide"))
    band = psi_band.shape[0]
    starts = [pl.multiple_of((here ^ shift) * band, band) for shift in order]

    total[...] = jnp.zeros_like(total)
    ph[NEAR], pl_[NEAR] = split(keep(near[...], lcounts[NEAR], rcounts[NEAR]))
    whole.wait()
    masked = keep(sbuf[...], lcounts[OWN], rcounts[OWN])
    ph[OWN], pl_[OWN] = split(masked)
    norm[...] = jnp.full(norm.shape, jnp.sum(masked * masked), F32)
    sbuf[...] = masked
    psi_band[...] = sbuf[pl.ds(pl.multiple_of(here * band, band), band), :]
    for p, start in enumerate(starts):
        psi[p * band : (p + 1) * band, :] = sbuf[pl.ds(start, band), :]

    for j in range(chans):
        kind = sum(jnp.where(places[c] == j, kinds[c], 0) for c in range(chans))
        lcount, rcount = pick(lcounts, kind), pick(rcounts, kind)
        for copy in copies[j]:
            copy.wait()

        def halve():
            rh[j], rl[j] = split(keep(rbuf[j], rcounts[OWN], rcount))
            for p, start in enumerate(starts):
                rows = slice(p * band, (p + 1) * band)
                piece = keep(lbuf[j, pl.ds(start, band), :], lcounts[OWN], lcount, start)
                lh[j, rows, :], ll[j, rows, :] = split(piece)

        @pl.when(kind <= NEAR)
        def _():
            halve()
            y = split(product((ph[kind], pl_[kind]), (rh[j], rl[j]), NT))
            total[...] += product((lh[j], ll[j]), y, NN)

        @pl.when(kind > NEAR)
        def _():
            halve()


def over_far(table, chans, group):
    first, have = table[0, 2], table[0, 3] - table[0, 2]
    for count in range(1, chans + 1):

        @pl.when(have == count)
        def _():
            group([first + i for i in range(count)])


def far_kernel(table, far, lh, ll, rh, rl, before, total, ph, pl_):
    rows = far.shape[0]

    @pl.when(table[0, 3] > table[0, 2])
    def _():
        ph[...], pl_[...] = split(keep(far[...], table[0, 0], table[0, 1]))

        def group(slots):
            psi = (ph[...], pl_[...])
            ys = [split(product(psi, (rh[j], rl[j]), NT)) for j in slots]
            terms = [product((lh[j, :, :rows], ll[j, :, :rows]), y, NN) for j, y in zip(slots, ys)]
            total[...] += functools.reduce(jnp.add, terms)

        over_far(table, lh.shape[0], group)


def last_kernel(table, far, lh, ll, rh, rl, before, psi, norm, *rest):
    *outs, total, ph, pl_ = rest
    rows = far.shape[0]
    block = psi.shape[0]

    @pl.when(table[0, 3] == table[0, 2])
    def _():
        total[...] = before[...]

    @pl.when(table[0, 3] > table[0, 2])
    def _():
        ph[...], pl_[...] = split(keep(far[...], table[0, 0], table[0, 1], block - rows))

        def group(slots):
            psi_far = (ph[...], pl_[...])
            ys = [split(product(psi_far, (rh[j], rl[j]), NT)) for j in slots]
            terms = [
                product((lh[j, :, block - rows :], ll[j, :, block - rows :]), y, NN) for j, y in zip(slots, ys)
            ]
            total[...] = before[...] + functools.reduce(jnp.add, terms)

        over_far(table, lh.shape[0], group)

    row = lax.broadcasted_iota(jnp.int32, (TAIL, block), 0)
    sums = jnp.where(row == 0, jnp.sum(psi[...] * total[...]), norm[0, 0])
    size = outs[0].shape[0] - TAIL
    for i, out in enumerate(outs):
        out[:size, :] = total[i * size : (i + 1) * size, :]
        out[size:, :] = sums


def add_kernel(*refs):
    *parts, out = refs
    whole = parts[0][...]
    for part in parts[1:]:
        whole += part[...]
    out[...] = whole


def add_first_kernel(*refs):
    *parts, out = refs
    whole = parts[0][...]
    for part in parts[1:]:
        whole += part[...]
    row = lax.broadcasted_iota(jnp.int32, out.shape, 0)
    out[...] = jnp.where(row == 0, whole, parts[0][...])


def merge_kernel(*refs):
    *parts, sums, mine, give = refs
    half = mine.shape[0]
    whole = parts[0][: 2 * half, :]
    tail = parts[0][2 * half :, :128]
    first = tail
    for part in parts[1:]:
        whole += part[: 2 * half, :]
        first += part[2 * half :, :128]
    mine[...] = whole[:half]
    give[...] = whole[half:]
    row = lax.broadcasted_iota(jnp.int32, sums.shape, 0)
    sums[...] = jnp.where(row == 0, first, tail)


def halves_kernel(*refs):
    *parts, mine, give = refs
    half = mine.shape[0]
    whole = parts[0][...]
    for part in parts[1:]:
        whole += part[...]
    mine[...] = whole[:half]
    give[...] = whole[half:]


def final_kernel(n_parts, psi, *rest):
    parts, (*sums, out, alpha) = rest[:n_parts], rest[n_parts:]
    both = sums[0][0:2, :]
    for more in sums[1:]:
        both += more[0:2, :]
    ratio = both[0:1, :] / both[1:2, :]
    share = parts[0][...]
    for part in parts[1:]:
        share += part[...]
    out[...] = share - jnp.concatenate([ratio] * (psi.shape[1] // ratio.shape[1]), axis=1) * psi[...]
    alpha[...] = ratio


def exchange(value, axis, shift):
    count = lax.axis_size(axis)
    return lax.ppermute(value, axis, [(i, i ^ shift) for i in range(count)])


def f32(*shape):
    return jax.ShapeDtypeStruct(shape, F32)


def cost(flops, size=2**20):
    return pl.CostEstimate(flops=flops, bytes_accessed=size, transcendentals=0)


def call(kernel, out_shape, n_in, scratch=(), name=None, **more):
    return pl.pallas_call(
        kernel,
        out_shape=out_shape,
        in_specs=[VMEM] * n_in,
        out_specs=jax.tree.map(lambda _: VMEM, out_shape),
        scratch_shapes=scratch,
        compiler_params=pltpu.CompilerParams(vmem_limit_bytes=16 * 2**20),
        name=name,
        **more,
    )


def per_device(state, left_env, right_env, left_sizes, right_sizes, channel_charge):
    chans, _, block, _ = left_env.shape
    n_wide, n_narrow = lax.axis_size("wide"), lax.axis_size("narrow")
    band, half = block // n_wide, block // 2
    own = state[0]
    square, small = f32(block, block), f32(8, 128)
    work = 6 * chans * block**3

    ends = [(0, 0), (n_narrow - 1, n_narrow - 1)]
    across = [pair for k in range(1, n_narrow - 1, 2) for pair in ((k, k + 1), (k + 1, k))]
    far_top, far_low = (lax.ppermute(rows, "narrow", across + ends) for rows in (own[:half], own[half:]))
    near = exchange(own, "narrow", 1)

    halves = jax.ShapeDtypeStruct((chans, block, block), BF16)
    table, psi, psi_band, norm, lh, ll, rh, rl, total = pl.pallas_call(
        main_kernel,
        out_shape=[jax.ShapeDtypeStruct((8, 128), jnp.int32), square, f32(band, block), small]
        + [halves] * 4
        + [square],
        in_specs=[HBM] * 6 + [VMEM],
        out_specs=[VMEM] * 9,
        scratch_shapes=[
            pltpu.SMEM(left_sizes.shape, jnp.int32),
            pltpu.SMEM(right_sizes.shape, jnp.int32),
            pltpu.SMEM(channel_charge.shape, jnp.int32),
            pltpu.VMEM((chans, block, block), F32),
            pltpu.VMEM((chans, block, block), F32),
            pltpu.VMEM((block, block), F32),
            pltpu.VMEM((2, block, block), BF16),
            pltpu.VMEM((2, block, block), BF16),
            pltpu.SemaphoreType.DMA((2, chans)),
            pltpu.SemaphoreType.DMA((4,)),
        ],
        compiler_params=pltpu.CompilerParams(vmem_limit_bytes=32 * 2**20),
        cost_estimate=cost(work, 8 * chans * block * block),
        name="main",
    )(
        left_sizes, right_sizes, channel_charge,
        *(pltpu.with_memory_space_constraint(x, pltpu.HBM) for x in (state, left_env, right_env)),
        near,
    )
    envs = (lh, ll, rh, rl)

    pair = [pltpu.VMEM((half, block), BF16)] * 2
    total = call(far_kernel, square, 7, pair, name="far", cost_estimate=cost(work), input_output_aliases={6: 0})(table, far_top, *envs, total)

    groups = min(4, n_wide)
    held = n_wide // groups
    blocks = call(
        last_kernel, [f32(held * band + TAIL, block)] * groups, 9, [pltpu.VMEM((block, block), F32)] + pair,
        name="last", cost_estimate=cost(work),
    )(table, far_low, *envs, total, psi, norm)
    parts = [blocks[0]] + [exchange(blocks[s], "wide", s) for s in range(groups - 1, 0, -1)]

    held //= 2
    sums, mine, give = call(merge_kernel, [small] + [f32(held * band, block)] * 2, groups, name="merge")(*parts)
    step = groups
    while step < n_wide:
        sums = call(add_first_kernel, small, 2, name="wide", cost_estimate=cost(16 * block**3))(sums, exchange(sums, "wide", step))
        step *= 2
    parts = [mine, exchange(give, "wide", groups * held)]
    while held > 1:
        held //= 2
        mine, give = call(halves_kernel, [f32(held * band, block)] * 2, 2, name="halves")(*parts)
        parts = [mine, exchange(give, "wide", groups * held)]
    others = []
    for step in [1] + ([3] if n_narrow >= 4 else []) + [1 << bit for bit in range(2, n_narrow.bit_length() - 1)]:
        if others:
            sums = call(add_kernel, small, 2, name="sectors")(sums, *others)
        others = [exchange(sums, "narrow", step)]

    out, alpha = call(
        functools.partial(final_kernel, len(parts)), [f32(band, block), f32(1, 128)], 2 + len(parts) + len(others),
        name="final",
    )(psi_band, *parts, sums, *others)
    return out[None], alpha[0, 0]


def solution(mesh):
    placed = (
        P("narrow", None, None),
        P("wide", "narrow", None, None),
        P("wide", "narrow", None, None),
        P(),
        P(),
        P("wide"),
    )
    return jax.shard_map(
        per_device,
        mesh=mesh,
        in_specs=placed,
        out_specs=(P("narrow", "wide", None), P()),
        check_vma=False,
    )
```
